256 devices in a mesh: section: 16 (over z, core), tensor: 4 (over y), dp: 4 (over x).
Axes of the slice: x: 4, y: 4, z: 8, core: 2. Of those that a mesh axis runs over, the one named last changes fastest.
Arguments:
- updates: bfloat16 [16, 64, 8192], P('section', 'dp', 'tensor')
- norm_gain: bfloat16 [8192], replicated, may hold values from 0.25 to 1.75
- head: bfloat16 [8192, 32000], P(None, ('section', 'tensor'))
- targets: int32 [64], P('dp'), may hold values from 0 to 31999
- curriculum: int32 [16], replicated, may hold values from 1 to 16
Outputs:
- update_grad: float32 [16, 64, 8192], P('section', 'dp', 'tensor')
- head_grad: bfloat16 [8192, 32000], P('dp', ('section', 'tensor'))
- section_losses: float32 [16], replicated
The draws below stay inside these ranges and needn't reach their ends.
Inputs may be any that keep to these rules, and one draw needn't show every extreme that they name: `curriculum`: numerators over a fixed denominator of 4.
All inputs are finite; a program needn't handle non-finite values.
Results may differ from the reference program's by a relative error of at most 0.013.
Values may be sent and summed in bfloat16 or wider, within the bound.
A program may use at most 128 MiB of HBM per device.

```python
import jax
import jax.numpy as jnp
from jax import lax

D = 8192
V = 32000
TOK = 16
TOKENS = 64
N_SECTION = 16
N_TENSOR = 4
N_DP = 4


def feature_pattern(key):
    pattern_key = jax.random.fold_in(key, 77)
    flips = jax.random.bernoulli(pattern_key, 0.5, (D,))
    return jnp.where(flips, 1.0, -1.0).astype(jnp.float32)


def draw_updates(key, part):
    pattern = feature_pattern(key)
    key = jax.random.fold_in(key, 11)
    noise_key, row_key = jax.random.split(key)
    shape = (N_SECTION, TOKENS, D)
    base = jax.random.normal(noise_key, shape, jnp.float32)
    feature = jnp.exp(jnp.log(10.0) * jnp.arange(D, dtype=jnp.float32) / D)
    row_scale = jnp.exp(jnp.log(10.0) * jax.random.uniform(row_key, (N_SECTION, TOKENS, 1), jnp.float32))
    values = 0.1 * base * feature * row_scale
    token_ids = jnp.arange(TOKENS)
    aligned = (token_ids % 5 == 0).astype(jnp.float32)
    sign_of = 1.0 - 2.0 * (token_ids // 5 % 2).astype(jnp.float32)
    level_table = jnp.array([0.15, 0.5, 2.0], jnp.float32)
    level = level_table[token_ids // 10 % 3]
    amplitude = (2.0 * aligned * sign_of * level)[None, :, None]
    values = values + amplitude * pattern[None, None, :] * row_scale
    return values.astype(jnp.bfloat16)


def draw_head(key, part):
    pattern = feature_pattern(key)
    key = jax.random.fold_in(key, 23)
    shape = (D, V)
    base = jax.random.normal(key, shape, jnp.float32)
    shared = 8.0
    column = jnp.exp(jnp.log(3.0) * jnp.arange(V, dtype=jnp.float32) / V)
    root_width = jnp.sqrt(jnp.float32(D))
    values = 1.2 * base * column[None, :] / root_width + shared / root_width
    columns = jnp.arange(V)
    leading = columns % 211
    strength = 120.0 * (1.0 + (columns // 211 % 3).astype(jnp.float32))
    boost = jnp.where(leading < 2, (strength - 2.0 * leading.astype(jnp.float32)) / jnp.float32(D), 0.0)
    values = values + pattern[:, None] * boost[None, :]
    return values.astype(jnp.bfloat16)


def touch_ends(values, own_key, smallest, high):
    spot = [jax.random.randint(jax.random.fold_in(own_key, axis), (), 0, length) for axis, length in enumerate(values.shape)]
    widest = values.shape.index(max(values.shape))
    neighbour = spot[:widest] + [(spot[widest] + 1) % values.shape[widest]] + spot[widest + 1:]
    return values.at[tuple(spot)].set(smallest).at[tuple(neighbour)].set(high)


def setup_inputs(seed: int = 0) -> dict:
    key_list = jax.random.split(jax.random.key(seed), 6)
    return {
        "updates": draw_updates(jax.random.fold_in(key_list[5], 71), 0),
        "norm_gain": jnp.clip(1.0 + 0.15 * jax.random.normal(key_list[1], (D,), jnp.float32), 0.25, 1.75).astype(jnp.bfloat16),
        "head": draw_head(jax.random.fold_in(key_list[5], 71), 0),
        "targets": touch_ends(jax.random.randint(key_list[3], (TOKENS,), 0, V), jax.random.fold_in(key_list[3], 1), 0, V - 1).astype(jnp.int32),
        "curriculum": touch_ends(jax.random.randint(key_list[4], (N_SECTION,), 1, 17), jax.random.fold_in(key_list[4], 1), 1, 16).astype(jnp.int32),
    }


epsilon = 1e-05
scale_denominator = 4.0

def reference(updates, norm_gain, head, targets, curriculum):
    hidden_state = jnp.cumsum(updates.astype(jnp.float32), axis=0)
    inverse_rms_scale = lax.rsqrt(lax.optimization_barrier(jnp.mean(hidden_state * hidden_state, axis=-1, keepdims=True)) + epsilon)
    norm_gain_vector = norm_gain.astype(jnp.float32)
    exit_rows = (norm_gain_vector * hidden_state * inverse_rms_scale).astype(jnp.bfloat16)
    rows_wide = exit_rows.astype(jnp.float32)
    width_blk = V // (N_SECTION * N_TENSOR)
    num_blocks = V // width_blk
    weights = curriculum.astype(jnp.float32) / scale_denominator

    def onehot_of(block_index):
        columns = block_index * width_blk + jnp.arange(width_blk, dtype=jnp.int32)
        return (columns[None, :] == targets[:, None]).astype(jnp.float32)

    def logits_of(block_index):
        head_blk = lax.dynamic_slice_in_dim(head, block_index * width_blk, width_blk, 1).astype(jnp.float32)
        return (jnp.einsum('sid,dv->siv', rows_wide, head_blk), head_blk)

    def stats(carried, block_index):
        top, summed, target_logit = carried
        logits_blk, head_blk = logits_of(block_index)
        new_top = jnp.maximum(top, lax.optimization_barrier(jnp.max(logits_blk, axis=-1)))
        summed = summed * jnp.exp(top - new_top) + lax.optimization_barrier(jnp.sum(jnp.exp(logits_blk - new_top[..., None]), axis=-1))
        target_logit = target_logit + lax.optimization_barrier(jnp.sum(logits_blk * onehot_of(block_index)[None], axis=-1))
        return ((new_top, summed, target_logit), None)
    start_top = jnp.full((N_SECTION, TOKENS), -jnp.inf, jnp.float32)
    zeros_rows = jnp.zeros((N_SECTION, TOKENS), jnp.float32)
    (top, summed, target_logit), _ = lax.scan(stats, (start_top, zeros_rows, zeros_rows), jnp.arange(num_blocks, dtype=jnp.int32))
    lse = top + jnp.log(summed)
    section_losses = lax.optimization_barrier(jnp.mean(lse - target_logit, axis=1))

    def backward(early_exit_gradient, block_index):
        logits_blk, head_blk = logits_of(block_index)
        probs = jnp.exp(logits_blk - lse[..., None])
        grad_blk = (weights[:, None, None] * (probs - onehot_of(block_index)[None])).astype(jnp.bfloat16)
        grad_wide = grad_blk.astype(jnp.float32)
        early_exit_gradient = early_exit_gradient + jnp.einsum('siv,dv->sid', grad_wide, head_blk)
        rows_split = rows_wide.reshape(N_SECTION, N_DP, TOK, D)
        grad_split = grad_wide.reshape(N_SECTION, N_DP, TOK, width_blk)
        replica = jnp.einsum('srid,sriv->rdv', rows_split, grad_split).astype(jnp.bfloat16)
        replica = lax.optimization_barrier(replica)
        head_blk_grad = lax.optimization_barrier(jnp.sum(replica.astype(jnp.float32), axis=0)).astype(jnp.bfloat16)
        return (early_exit_gradient, head_blk_grad)
    early_exit_gradient, head_parts = lax.scan(backward, jnp.zeros((N_SECTION, TOKENS, D), jnp.float32), jnp.arange(num_blocks, dtype=jnp.int32))
    head_grad = jnp.moveaxis(head_parts, 0, 1).reshape(D, V)
    normalized_hidden = hidden_state * inverse_rms_scale
    projected_rows = lax.optimization_barrier(jnp.mean(norm_gain_vector * early_exit_gradient * normalized_hidden, axis=-1, keepdims=True))
    hidden_state_gradient = inverse_rms_scale * (norm_gain_vector * early_exit_gradient - normalized_hidden * projected_rows)
    update_grad = jnp.flip(jnp.cumsum(jnp.flip(hidden_state_gradient, 0), axis=0), 0)
    return (update_grad, head_grad, section_losses)
```

```python
import jax
import jax.numpy as jnp
from jax import lax
from jax.experimental import pallas as pl
from jax.experimental.pallas import tpu as pltpu
from jax.sharding import PartitionSpec as P

F32 = jnp.float32
BF16 = jnp.bfloat16
epsilon = 1e-05
scale_denominator = 4.0

NY = 4
NX = 4
NZ = 8

GATHER_Y = (0, -1, 1, 2)
SCATTER_Y = (2, 1, -1, 0)
SCATTER_Z = (4, 3, -3, 2, -2, 1, -1, 0)


def wrap(value, count):
    return lax.rem(value + 2 * count, count)


def kernel(
    upd, gain, head, targets, curriculum,
    upd_grad, head_grad, losses,
    U, H, R, PB, SB, RB, RX, GX, L, SQ, INV, COEF, ST1, ST2, ST3, CT1, CT2, CT3, NL,
    local_sem, r_own, r_sib, s_sib, s_p, s_m, s_y,
    s_st, r_st1, r_st2, r_st3, s_ct, r_ct1, r_ct2, r_ct3, s_nl, r_nl,
    s_rx, r_rx, s_rxs, r_rxs, s_g, r_g, s_sb, r_sb, s_rs, r_rs,
):
    tok, q = upd.shape[1], upd.shape[2]
    width = q * NY
    vdev = head.shape[1]
    half = NZ * tok
    rows = 2 * half
    s = lax.axis_index("section")
    y = lax.axis_index("tensor")
    x = lax.axis_index("dp")
    core = lax.rem(s, 2)
    z = lax.div(s, 2)
    sibling = s + 1 - 2 * core

    def copy_to(src, dst, ssem, rsem, **device):
        return pltpu.make_async_remote_copy(
            src_ref=src, dst_ref=dst, send_sem=ssem, recv_sem=rsem,
            device_id=device, device_id_type=pl.DeviceIdType.MESH,
        )

    def arrived(dst, rsem):
        copy_to(dst, dst, local_sem.at[0], rsem, section=sibling).wait_recv()

    def at_z(zz):
        return 2 * wrap(zz, NZ) + core

    def block_rows(cc, zz):
        return pl.ds(pl.multiple_of((cc * NZ + zz) * tok, tok), tok)

    def slice_y(yy):
        return pl.ds(pl.multiple_of(yy * q, q), q)

    def half_rows(cc):
        return pl.ds(pl.multiple_of(cc * half, half), half)

    barrier = pltpu.get_barrier_semaphore()
    peers = [dict(section=sibling)]
    peers += [dict(tensor=wrap(y + d, NY)) for d in range(1, NY)]
    peers += [dict(section=at_z(z + d)) for d in range(1, NZ)]
    peers += [dict(dp=wrap(x + d, NX)) for d in range(1, NX)]
    for peer in peers:
        pl.semaphore_signal(barrier, inc=1, device_id=peer, device_id_type=pl.DeviceIdType.MESH)
    load_head = pltpu.make_async_copy(head, H, local_sem.at[1])
    load_head.start()
    pl.semaphore_wait(barrier, len(peers))

    own = upd.at[0]

    def ublk(cc, zz, yy):
        return U.at[block_rows(cc, zz), slice_y(yy)]

    keep_own = pltpu.make_async_copy(own, ublk(core, z, y), local_sem.at[2])
    keep_own.start()

    @pl.when(core == 0)
    def _():
        copies = []

        def pass_on(src, zz, yy, k, j):
            dst = ublk(0, zz, yy)
            near = k + 1 < NZ // 2
            if k >= 0 and (near or (k + 1 == NZ // 2 and j < NY // 2)) and src[1] != "right":
                copies.append(copy_to(src[0], dst, s_p.at[k, j], r_own.at[zz, yy], section=at_z(z + 1)))
                copies[-1].start()
            if k >= 0 and (near or (k + 1 == NZ // 2 and j >= NY // 2)) and src[1] != "left":
                copies.append(copy_to(src[0], dst, s_m.at[k, j], r_own.at[zz, yy], section=at_z(z - 1)))
                copies[-1].start()
            copies.append(copy_to(src[0], dst, s_sib.at[zz, yy], r_sib.at[zz, yy], section=sibling))
            copies[-1].start()

        for n, d in enumerate((1, -1, 2)):
            copies.append(copy_to(own, ublk(0, z, y), s_y.at[n, 0], r_own.at[z, y], tensor=wrap(y + d, NY)))
            copies[-1].start()
        pass_on((own, "here"), z, y, 0, 0)
        for j in range(1, NY):
            yy = wrap(y + GATHER_Y[j], NY)
            arrived(ublk(0, z, yy), r_own.at[z, yy])
            pass_on((ublk(0, z, yy), "here"), z, yy, 0, j)
        for k in range(1, NZ // 2 + 1):
            for j in range(NY):
                yy = wrap(y + GATHER_Y[j], NY)
                if k < NZ // 2 or j < NY // 2:
                    zz = wrap(z - k, NZ)
                    arrived(ublk(0, zz, yy), r_own.at[zz, yy])
                    pass_on((ublk(0, zz, yy), "left"), zz, yy, k, j)
                if k < NZ // 2 or j >= NY // 2:
                    zz = wrap(z + k, NZ)
                    arrived(ublk(0, zz, yy), r_own.at[zz, yy])
                    pass_on((ublk(0, zz, yy), "right"), zz, yy, k, j)
        for copy in copies:
            copy.wait_send()

    @pl.when(core == 1)
    def _():
        copies = []
        order = [(0, "here")]
        for k in range(1, NZ // 2):
            order += [(-k, "left"), (k, "right")]
        order += [(-(NZ // 2), "left")]

        def to_sibling(zz, yy, src):
            copies.append(copy_to(src, ublk(1, zz, yy), s_sib.at[zz, yy], r_sib.at[zz, yy], section=sibling))
            copies[-1].start()

        for n in range(len(order) + 2):
            if n < len(order):
                d, side = order[n]
                zz = wrap(z + d, NZ)
                dst = ublk(1, zz, y)
                src = own if n == 0 else dst
                if n > 0:
                    arrived(dst, r_own.at[zz, y])
                if side != "right" and abs(d) + 1 <= NZ // 2:
                    copies.append(copy_to(src, dst, s_p.at[abs(d), 0], r_own.at[zz, y], section=at_z(z + 1)))
                    copies[-1].start()
                if side != "left" and abs(d) + 1 < NZ // 2:
                    copies.append(copy_to(src, dst, s_m.at[abs(d), 0], r_own.at[zz, y], section=at_z(z - 1)))
                    copies[-1].start()
                for m, step in enumerate((1, -1)):
                    copies.append(copy_to(src, dst, s_y.at[m, n], r_own.at[zz, y], tensor=wrap(y + step, NY)))
                    copies[-1].start()
                to_sibling(zz, y, src)
            if 1 <= n <= len(order):
                zz = wrap(z + order[n - 1][0], NZ)
                for m, step in enumerate((-1, 1)):
                    yy = wrap(y + step, NY)
                    dst = ublk(1, zz, yy)
                    arrived(dst, r_own.at[zz, yy])
                    if (n - 1) % 2 == m:
                        copies.append(copy_to(dst, dst, s_y.at[2, n - 1], r_own.at[zz, yy], tensor=wrap(y - step, NY)))
                        copies[-1].start()
                    to_sibling(zz, yy, dst)
            if n >= 2:
                zz = wrap(z + order[n - 2][0], NZ)
                yy = wrap(y + 2, NY)
                arrived(ublk(1, zz, yy), r_own.at[zz, yy])
                to_sibling(zz, yy, ublk(1, zz, yy))
        for copy in copies:
            copy.wait_send()

    def wait_sibling(n, carry):
        zz, yy = lax.div(n, NY), lax.rem(n, NY)
        arrived(ublk(1 - core, zz, yy), r_sib.at[zz, yy])
        return carry

    lax.fori_loop(0, NZ * NY, wait_sibling, 0)
    keep_own.wait()

    chunk = 512
    groups = chunk // 128

    def section_rows(k):
        return pl.ds(((k % 2) * NZ + k // 2) * tok, tok)

    SQ[...] = jnp.zeros_like(SQ)

    def squares(f, carry):
        cols = pl.ds(pl.multiple_of(f * chunk, chunk), chunk)
        hidden = jnp.zeros((tok, chunk), F32)
        for k in range(2 * NZ):
            hidden = hidden + U[section_rows(k), cols].astype(F32)
            square = hidden * hidden
            part = square[:, :128]
            for g in range(1, groups):
                part = part + square[:, g * 128:(g + 1) * 128]
            SQ[section_rows(k), :] += part
        return carry

    lax.fori_loop(0, width // chunk, squares, 0)
    mean = jnp.sum(SQ[...], axis=1, keepdims=True) / width
    INV[...] = jnp.broadcast_to(lax.rsqrt(mean + epsilon), (rows, 128))

    def normalize(f, carry):
        cols = pl.ds(pl.multiple_of(f * chunk, chunk), chunk)
        scale = gain[:, cols].astype(F32)
        hidden = jnp.zeros((tok, chunk), F32)
        for k in range(2 * NZ):
            hidden = hidden + U[section_rows(k), cols].astype(F32)
            inverse = INV[section_rows(k), :]
            R[section_rows(k), cols] = (
                scale * hidden * jnp.concatenate([inverse] * groups, axis=1)
            ).astype(BF16)
        return carry

    lax.fori_loop(0, width // chunk, normalize, 0)

    part = width // NX

    def slice_x(xx):
        return pl.ds(pl.multiple_of(xx * part, part), part)

    def rx_rows(xx, cc):
        return pl.ds(pl.multiple_of(xx * rows + cc * half, half), half)

    def x_rows(xx):
        return pl.ds(pl.multiple_of(xx * rows, rows), rows)

    row_copies = []
    for n, d in enumerate((1, -1, 2)):
        xx = wrap(x + d, NX)
        row_copies.append(copy_to(
            R.at[half_rows(core), slice_x(xx)], RX.at[rx_rows(x, core), :],
            s_rx.at[n], r_rx.at[x], dp=xx,
        ))
        row_copies[-1].start()
    keep_rows = pltpu.make_async_copy(R.at[:, slice_x(x)], RX.at[x_rows(x), :], local_sem.at[3])
    keep_rows.start()

    load_head.wait()
    depth = 1024
    L[...] = jnp.zeros_like(L)

    def logits_step(f, carry):
        cols = pl.ds(pl.multiple_of(f * depth, depth), depth)
        L[...] += jnp.dot(R[:, cols], H[cols, :], preferred_element_type=F32)
        return carry

    lax.fori_loop(0, width // depth, logits_step, 0)

    first = (s * NY + y) * vdev
    token = lax.broadcasted_iota(jnp.int32, (tok, vdev), 0)
    wanted = jnp.zeros((tok, vdev), jnp.int32)
    for i in range(tok):
        wanted = jnp.where(token == i, targets[i], wanted)
    hit = lax.broadcasted_iota(jnp.int32, (tok, vdev), 1) + first == wanted
    lane = lax.broadcasted_iota(jnp.int32, (tok, 128), 1)
    stats = []
    for b in range(2 * NZ):
        block = L[b * tok:(b + 1) * tok, :]
        top = jnp.max(block, axis=1, keepdims=True)
        total = jnp.sum(jnp.exp(block - top), axis=1, keepdims=True)
        target = jnp.sum(jnp.where(hit, block, 0.0), axis=1, keepdims=True)
        stats.append(jnp.where(lane == 0, top, jnp.where(lane == 1, total, target)))
    ST1[core] = jnp.transpose(jnp.concatenate(stats, axis=0))[:8]

    def combine(parts):
        top = parts[0][0:1]
        for p in parts[1:]:
            top = jnp.maximum(top, p[0:1])
        total = parts[0][1:2] * jnp.exp(parts[0][0:1] - top)
        target = parts[0][2:3]
        for p in parts[1:]:
            total = total + p[1:2] * jnp.exp(p[0:1] - top)
            target = target + p[2:3]
        return jnp.concatenate([top, total, target, jnp.zeros((5, rows), F32)], axis=0)

    def add_up(parts):
        total = parts[0]
        for p in parts[1:]:
            total = total + p
        return total

    def exchange(level, B1, B2, B3, ssem, r1, r2, r3):
        if level == 1:
            out = [copy_to(B1.at[core], B1.at[core], ssem.at[0], r1.at[core], section=sibling)]
        elif level == 2:
            out = [
                copy_to(B2.at[y], B2.at[y], ssem.at[n + 1], r2.at[y], tensor=wrap(y + d, NY))
                for n, d in enumerate((2, 1, 3))
            ]
        else:
            out = [
                copy_to(B3.at[z], B3.at[z], ssem.at[n + NY], r3.at[z], section=at_z(z + d))
                for n, d in enumerate((4, 3, 5, 2, 6, 1, 7))
            ]
        for copy in out:
            copy.start()
        return out

    def collect(level, B1, B2, B3, r1, r2, r3):
        if level == 1:
            arrived(B1.at[1 - core], r1.at[1 - core])
            return [B1[k] for k in range(2)]
        if level == 2:
            for d in (1, 3, 2):
                arrived(B2.at[wrap(y + d, NY)], r2.at[wrap(y + d, NY)])
            return [B2[k] for k in range(NY)]
        for d in (1, 7, 2, 6, 3, 5, 4):
            arrived(B3.at[wrap(z + d, NZ)], r3.at[wrap(z + d, NZ)])
        return [B3[k] for k in range(NZ)]

    small = []
    stat_bufs, stat_sems = (ST1, ST2, ST3), (r_st1, r_st2, r_st3)
    small += exchange(1, *stat_bufs, s_st, *stat_sems)
    ST2[y] = combine(collect(1, *stat_bufs, *stat_sems))
    small += exchange(2, *stat_bufs, s_st, *stat_sems)
    ST3[z] = combine(collect(2, *stat_bufs, *stat_sems))
    small += exchange(3, *stat_bufs, s_st, *stat_sems)
    final = combine(collect(3, *stat_bufs, *stat_sems))
    lse_row = final[0:1] + jnp.log(final[1:2])
    NL[x] = jnp.broadcast_to(lse_row - final[2:3], (8, rows))
    for n, d in enumerate((1, 2, 3)):
        small.append(copy_to(NL.at[x], NL.at[x], s_nl.at[n], r_nl.at[x], dp=wrap(x + d, NX)))
        small[-1].start()
    lse = jnp.transpose(jnp.broadcast_to(lse_row, (128, rows)))[:, 0:1]

    inner = []
    for b in range(2 * NZ):
        block = L[b * tok:(b + 1) * tok, :]
        weight = curriculum[(b % NZ) * 2 + b // NZ].astype(F32) / scale_denominator
        probs = jnp.exp(block - lse[b * tok:(b + 1) * tok])
        grad = (weight * (probs - jnp.where(hit, 1.0, 0.0))).astype(BF16)
        GX[pl.ds(pl.multiple_of(x * rows + b * tok, tok), tok), :] = grad
        product = jnp.sum(grad.astype(F32) * block, axis=1, keepdims=True)
        inner.append(jnp.broadcast_to(product, (tok, 128)))
    CT1[core] = jnp.transpose(jnp.concatenate(inner, axis=0))[:8]
    inner_bufs, inner_sems = (CT1, CT2, CT3), (r_ct1, r_ct2, r_ct3)
    small += exchange(1, *inner_bufs, s_ct, *inner_sems)
    for n, d in enumerate((1, -1, 2)):
        row_copies.append(copy_to(
            GX.at[x_rows(x), :], GX.at[x_rows(x), :], s_g.at[n], r_g.at[x], dp=wrap(x + d, NX)
        ))
        row_copies[-1].start()

    sib_copies = []
    for j in range(NY):
        yy = wrap(y + SCATTER_Y[j], NY)

        def share(f, carry):
            cols = pl.ds(pl.multiple_of(yy * q + f * chunk, chunk), chunk)
            term = lax.dot_general(
                GX[x_rows(x), :], H[cols, :], (((1,), (1,)), ((), ())), preferred_element_type=F32
            )
            later = jnp.zeros((tok, chunk), F32)
            for k in reversed(range(2 * NZ)):
                at = ((k % 2) * NZ + k // 2) * tok
                inverse = INV[section_rows(k), :]
                later = later + term[at:at + tok] * jnp.concatenate([inverse] * groups, axis=1)
                PB[section_rows(k), cols] = later
            return carry

        lax.fori_loop(0, q // chunk, share, 0)
        sib_copies.append(copy_to(
            PB.at[half_rows(1 - core), slice_y(yy)], SB.at[:, slice_y(yy)],
            s_sb.at[j], r_sb.at[j], section=sibling,
        ))
        sib_copies[-1].start()
        if j == 0:
            CT2[y] = add_up(collect(1, *inner_bufs, *inner_sems))
            small += exchange(2, *inner_bufs, s_ct, *inner_sems)
        if j == 2:
            CT3[z] = add_up(collect(2, *inner_bufs, *inner_sems))
            small += exchange(3, *inner_bufs, s_ct, *inner_sems)

    projected = add_up(collect(3, *inner_bufs, *inner_sems))[0:1]
    projected = jnp.transpose(jnp.broadcast_to(projected, (128, rows)))
    COEF[...] = INV[...] * INV[...] * projected / width

    def second_term(f, carry):
        cols = pl.ds(pl.multiple_of(y * q + f * chunk, chunk), chunk)
        hidden = jnp.zeros((tok, chunk), F32)
        later = jnp.zeros((tok, chunk), F32)
        for k in range(2 * NZ):
            hidden = hidden + U[section_rows(k), cols].astype(F32)
            factor = jnp.where(k >= s, COEF[section_rows(k), :], 0.0)
            later = later + hidden * jnp.concatenate([factor] * groups, axis=1)
        upd_grad[0, :, pl.ds(pl.multiple_of(f * chunk, chunk), chunk)] = later
        return carry

    lax.fori_loop(0, q // chunk, second_term, 0)
    own_gain = gain[:, slice_y(y)].astype(F32)

    def held(cc, zz, yy):
        return PB.at[block_rows(cc, zz), slice_y(yy)]

    def pair_sum(cc, zz, yy):
        return PB[block_rows(cc, zz), slice_y(yy)] + SB[pl.ds(pl.multiple_of(zz * tok, tok), tok), slice_y(yy)]

    @pl.when(core == 0)
    def _():
        copies = []
        up = lambda o, j: o * NY + j
        down = lambda o, j: (NZ // 2 + o) * NY + j
        last = NZ * NY

        def ring(o, j, sign, slot):
            zz = wrap(z + sign * o, NZ)
            yy = wrap(y + SCATTER_Y[j], NY)
            total = pair_sum(0, zz, yy)
            first_half = (j < NY // 2) == (sign > 0)
            if o + 1 < NZ // 2 or (o + 1 == NZ // 2 and first_half):
                arrived(RB.at[slot(o, j)], r_rs.at[slot(o, j)])
                total = total + RB[slot(o, j)]
            PB[block_rows(0, zz), slice_y(yy)] = total
            copies.append(copy_to(
                held(0, zz, yy), RB.at[slot(o - 1, j)], s_rs.at[slot(o - 1, j)], r_rs.at[slot(o - 1, j)],
                section=at_z(z + sign),
            ))
            copies[-1].start()

        for o in range(NZ // 2, 0, -1):
            for j in range(NY):
                if o == NZ // 2:
                    arrived(SB.at[:, slice_y(wrap(y + SCATTER_Y[j], NY))], r_sb.at[j])
                if o < NZ // 2 or j < NY // 2:
                    ring(o, j, 1, up)
                if o < NZ // 2 or j >= NY // 2:
                    ring(o, j, -1, down)
        for j in range(NY):
            yy = wrap(y + SCATTER_Y[j], NY)
            arrived(RB.at[up(0, j)], r_rs.at[up(0, j)])
            arrived(RB.at[down(0, j)], r_rs.at[down(0, j)])
            total = pair_sum(0, z, yy) + RB[up(0, j)] + RB[down(0, j)]
            if j < NY - 1:
                PB[block_rows(0, z), slice_y(yy)] = total
                copies.append(copy_to(
                    held(0, z, yy), RB.at[last + j], s_rs.at[last + j], r_rs.at[last + j], tensor=yy
                ))
                copies[-1].start()
        for j in (1, 2, 0):
            arrived(RB.at[last + j], r_rs.at[last + j])
            total = total + RB[last + j]
        upd_grad[0] = own_gain * total - upd_grad[0]
        for copy in copies:
            copy.wait_send()

    @pl.when(core == 1)
    def _():
        copies = []
        count = len(SCATTER_Z)
        far, plus, minus = 0, count, 2 * count
        zplus, zminus = 3 * count, 3 * count + NZ // 2

        def send(src, slot, **device):
            copies.append(copy_to(src, RB.at[slot], s_rs.at[slot], r_rs.at[slot], **device))
            copies[-1].start()

        for j in range(NY):
            yy = wrap(y + SCATTER_Y[j], NY)
            arrived(SB.at[:, slice_y(yy)], r_sb.at[j])
            for n in range(count):
                zz = wrap(z + SCATTER_Z[n], NZ)
                total = pair_sum(1, zz, yy)
                if j == 0:
                    PB[block_rows(1, zz), slice_y(yy)] = total
                    send(held(1, zz, yy), far + n, tensor=wrap(y + (1 if n % 2 == 0 else -1), NY))
                elif j < NY - 1:
                    step = SCATTER_Y[j]
                    if (n % 2 == 0) == (step == 1):
                        arrived(RB.at[far + n], r_rs.at[far + n])
                        total = total + RB[far + n]
                    PB[block_rows(1, zz), slice_y(yy)] = total
                    send(held(1, zz, yy), (plus if step == 1 else minus) + n, tensor=yy)
                else:
                    arrived(RB.at[plus + n], r_rs.at[plus + n])
                    arrived(RB.at[minus + n], r_rs.at[minus + n])
                    total = total + RB[plus + n] + RB[minus + n]
                    o = SCATTER_Z[n]
                    if o == 0:
                        arrived(RB.at[zplus], r_rs.at[zplus])
                        arrived(RB.at[zminus], r_rs.at[zminus])
                        total = total + RB[zplus] + RB[zminus]
                        upd_grad[0] = own_gain * total - upd_grad[0]
                    else:
                        base, sign = (zplus, 1) if o > 0 else (zminus, -1)
                        depth_here = abs(o)
                        if depth_here < (NZ // 2 if o > 0 else NZ // 2 - 1):
                            arrived(RB.at[base + depth_here], r_rs.at[base + depth_here])
                            total = total + RB[base + depth_here]
                        PB[block_rows(1, zz), slice_y(yy)] = total
                        send(held(1, zz, yy), base + depth_here - 1, section=at_z(z + sign))
        for copy in copies:
            copy.wait_send()

    keep_rows.wait()
    for d in (1, -1, 2):
        xx = wrap(x + d, NX)
        dst = RX.at[rx_rows(xx, core), :]
        arrived(dst, r_rx.at[xx])
        row_copies.append(copy_to(dst, dst, s_rxs.at[xx], r_rxs.at[xx], section=sibling))
        row_copies[-1].start()
    for d in (1, -1, 2):
        xx = wrap(x + d, NX)
        arrived(GX.at[x_rows(xx), :], r_g.at[xx])
        arrived(RX.at[rx_rows(xx, 1 - core), :], r_rxs.at[xx])
        arrived(NL.at[xx], r_nl.at[xx])

    def head_part(f, carry):
        cols = pl.ds(pl.multiple_of(f * 256, 256), 256)
        head_grad[cols, :] = lax.dot_general(
            RX[:, cols], GX[...], (((0,), (0,)), ((), ())), preferred_element_type=F32
        ).astype(BF16)
        return carry

    lax.fori_loop(0, part // 256, head_part, 0)

    nll = add_up([NL[k] for k in range(NX)])
    nll = jnp.transpose(jnp.broadcast_to(nll[0:1], (128, rows)))
    for b in range(2 * NZ):
        section = (b % NZ) * 2 + b // NZ
        losses[section:section + 1, :] = jnp.sum(
            nll[b * tok:(b + 1) * tok], axis=0, keepdims=True
        ) / (tok * NX)

    for copy in row_copies + sib_copies + small:
        copy.wait_send()


def body(updates, norm_gain, head, targets, curriculum):
    _, tok, q = updates.shape
    width, vdev = head.shape
    rows = 2 * NZ * tok
    vmem = pl.BlockSpec(memory_space=pltpu.VMEM)
    smem = pl.BlockSpec(memory_space=pltpu.SMEM)
    dma = lambda *shape: pltpu.SemaphoreType.DMA(shape)
    slots = NZ * NY + NY
    upd_grad, head_grad, losses = pl.pallas_call(
        kernel,
        out_shape=(
            jax.ShapeDtypeStruct((1, tok, q), F32),
            jax.ShapeDtypeStruct((width // NX, vdev), BF16),
            jax.ShapeDtypeStruct((2 * NZ, 128), F32),
        ),
        in_specs=[vmem, vmem, pl.BlockSpec(memory_space=pl.ANY), smem, smem],
        out_specs=(vmem, vmem, vmem),
        scratch_shapes=[
            pltpu.VMEM((rows, width), BF16),
            pltpu.VMEM((width, vdev), BF16),
            pltpu.VMEM((rows, width), BF16),
            pltpu.VMEM((rows, width), F32),
            pltpu.VMEM((rows // 2, width), F32),
            pltpu.VMEM((slots, tok, q), F32),
            pltpu.VMEM((NX * rows, width // NX), BF16),
            pltpu.VMEM((NX * rows, vdev), BF16),
            pltpu.VMEM((rows, vdev), F32),
            pltpu.VMEM((rows, 128), F32),
            pltpu.VMEM((rows, 128), F32),
            pltpu.VMEM((rows, 128), F32),
            pltpu.VMEM((2, 8, rows), F32),
            pltpu.VMEM((NY, 8, rows), F32),
            pltpu.VMEM((NZ, 8, rows), F32),
            pltpu.VMEM((2, 8, rows), F32),
            pltpu.VMEM((NY, 8, rows), F32),
            pltpu.VMEM((NZ, 8, rows), F32),
            pltpu.VMEM((NX, 8, rows), F32),
            dma(4), dma(NZ, NY), dma(NZ, NY), dma(NZ, NY), dma(NZ, NY), dma(NZ, NY), dma(3, NZ),
            dma(NY + NZ), dma(2), dma(NY), dma(NZ), dma(NY + NZ), dma(2), dma(NY), dma(NZ), dma(NX), dma(NX),
            dma(NX), dma(NX), dma(NX), dma(NX), dma(NX), dma(NX), dma(NY), dma(NY), dma(slots), dma(slots),
        ],
        compiler_params=pltpu.CompilerParams(
            collective_id=0, has_side_effects=True, vmem_limit_bytes=60 * 1024 * 1024
        ),
    )(updates, norm_gain.reshape(1, width), head, targets, curriculum)
    return upd_grad, head_grad, losses[:, 0]


def solution(mesh):
    return jax.shard_map(
        body,
        mesh=mesh,
        in_specs=(P("section", "dp", "tensor"), P(), P(None, ("section", "tensor")), P("dp"), P()),
        out_specs=(P("section", "dp", "tensor"), P("dp", ("section", "tensor")), P()),
        check_vma=False,
    )
```

```python
import jax
import jax.numpy as jnp
from jax import lax
from jax.experimental import pallas as pl
from jax.experimental.pallas import tpu as pltpu
from jax.sharding import PartitionSpec as P

F32 = jnp.float32
BF16 = jnp.bfloat16
epsilon = 1e-05
scale_denominator = 4.0

NY = 4
NX = 4
NZ = 8

GATHER_Y = (0, -1, 1, 2)
SCATTER_Y = (2, 1, -1, 0)
SCATTER_Z = (4, 3, -3, 2, -2, 1, -1, 0)


def wrap(value, count):
    return lax.rem(value + 2 * count, count)


def kernel(
    upd, gain, head, targets, curriculum,
    upd_grad, head_grad, losses,
    U, H, R, PB, SB, RB, RX, GX, GN, L, GAIN, SQ, INV, COEF, ST1, ST2, ST3, CT1, CT2, CT3, NL,
    local_sem, r_own, r_sib, s_sib, s_p, s_m, s_y,
    s_st, r_st1, r_st2, r_st3, s_ct, r_ct1, r_ct2, r_ct3, s_nl, r_nl,
    s_rx, r_rx, s_rxs, r_rxs, s_g, r_g, s_sb, r_sb, s_rs, r_rs,
):
    tok, q = upd.shape[1], upd.shape[2]
    width = q * NY
    vdev = head.shape[0]
    vpad = L.shape[0]
    half = NZ * tok
    rows = 2 * half
    s = lax.axis_index("section")
    y = lax.axis_index("tensor")
    x = lax.axis_index("dp")
    core = lax.rem(s, 2)
    z = lax.div(s, 2)
    sibling = s + 1 - 2 * core

    def copy_to(src, dst, ssem, rsem, **device):
        return pltpu.make_async_remote_copy(
            src_ref=src, dst_ref=dst, send_sem=ssem, recv_sem=rsem,
            device_id=device, device_id_type=pl.DeviceIdType.MESH,
        )

    def arrived(dst, rsem):
        copy_to(dst, dst, local_sem.at[0], rsem, section=sibling).wait_recv()

    def at_z(zz):
        return 2 * wrap(zz, NZ) + core

    def block_rows(cc, zz):
        return pl.ds(pl.multiple_of((cc * NZ + zz) * tok, tok), tok)

    def slice_y(yy):
        return pl.ds(pl.multiple_of(yy * q, q), q)

    def half_rows(cc):
        return pl.ds(pl.multiple_of(cc * half, half), half)

    barrier = pltpu.get_barrier_semaphore()
    peers = [dict(section=sibling)]
    peers += [dict(tensor=wrap(y + d, NY)) for d in range(1, NY)]
    peers += [dict(section=at_z(z + d)) for d in range(1, NZ)]
    peers += [dict(dp=wrap(x + d, NX)) for d in range(1, NX)]
    for peer in peers:
        pl.semaphore_signal(barrier, inc=1, device_id=peer, device_id_type=pl.DeviceIdType.MESH)
    load_head = pltpu.make_async_copy(head, H, local_sem.at[1])
    load_head.start()
    pl.semaphore_wait(barrier, len(peers))

    own = upd.at[0]

    def ublk(cc, zz, yy):
        return U.at[block_rows(cc, zz), slice_y(yy)]

    keep_own = pltpu.make_async_copy(own, ublk(core, z, y), local_sem.at[2])
    keep_own.start()

    @pl.when(core == 0)
    def _():
        copies = []

        def pass_on(src, zz, yy, k, j):
            dst = ublk(0, zz, yy)
            near = k + 1 < NZ // 2
            if k >= 0 and (near or (k + 1 == NZ // 2 and j < NY // 2)) and src[1] != "right":
                copies.append(copy_to(src[0], dst, s_p.at[k, j], r_own.at[zz, yy], section=at_z(z + 1)))
                copies[-1].start()
            if k >= 0 and (near or (k + 1 == NZ // 2 and j >= NY // 2)) and src[1] != "left":
                copies.append(copy_to(src[0], dst, s_m.at[k, j], r_own.at[zz, yy], section=at_z(z - 1)))
                copies[-1].start()
            copies.append(copy_to(src[0], dst, s_sib.at[zz, yy], r_sib.at[zz, yy], section=sibling))
            copies[-1].start()

        for n, d in enumerate((1, -1, 2)):
            copies.append(copy_to(own, ublk(0, z, y), s_y.at[n, 0], r_own.at[z, y], tensor=wrap(y + d, NY)))
            copies[-1].start()
        pass_on((own, "here"), z, y, 0, 0)
        for j in range(1, NY):
            yy = wrap(y + GATHER_Y[j], NY)
            arrived(ublk(0, z, yy), r_own.at[z, yy])
            pass_on((ublk(0, z, yy), "here"), z, yy, 0, j)
        for k in range(1, NZ // 2 + 1):
            for j in range(NY):
                yy = wrap(y + GATHER_Y[j], NY)
                if k < NZ // 2 or j < NY // 2:
                    zz = wrap(z - k, NZ)
                    arrived(ublk(0, zz, yy), r_own.at[zz, yy])
                    pass_on((ublk(0, zz, yy), "left"), zz, yy, k, j)
                if k < NZ // 2 or j >= NY // 2:
                    zz = wrap(z + k, NZ)
                    arrived(ublk(0, zz, yy), r_own.at[zz, yy])
                    pass_on((ublk(0, zz, yy), "right"), zz, yy, k, j)
        for copy in copies:
            copy.wait_send()

    @pl.when(core == 1)
    def _():
        copies = []
        order = [(0, "here")]
        for k in range(1, NZ // 2):
            order += [(-k, "left"), (k, "right")]
        order += [(-(NZ // 2), "left")]

        def to_sibling(zz, yy, src):
            copies.append(copy_to(src, ublk(1, zz, yy), s_sib.at[zz, yy], r_sib.at[zz, yy], section=sibling))
            copies[-1].start()

        for n in range(len(order) + 2):
            if n < len(order):
                d, side = order[n]
                zz = wrap(z + d, NZ)
                dst = ublk(1, zz, y)
                src = own if n == 0 else dst
                if n > 0:
                    arrived(dst, r_own.at[zz, y])
                if side != "right" and abs(d) + 1 <= NZ // 2:
                    copies.append(copy_to(src, dst, s_p.at[abs(d), 0], r_own.at[zz, y], section=at_z(z + 1)))
                    copies[-1].start()
                if side != "left" and abs(d) + 1 < NZ // 2:
                    copies.append(copy_to(src, dst, s_m.at[abs(d), 0], r_own.at[zz, y], section=at_z(z - 1)))
                    copies[-1].start()
                for m, step in enumerate((1, -1)):
                    copies.append(copy_to(src, dst, s_y.at[m, n], r_own.at[zz, y], tensor=wrap(y + step, NY)))
                    copies[-1].start()
                to_sibling(zz, y, src)
            if 1 <= n <= len(order):
                zz = wrap(z + order[n - 1][0], NZ)
                for m, step in enumerate((-1, 1)):
                    yy = wrap(y + step, NY)
                    dst = ublk(1, zz, yy)
                    arrived(dst, r_own.at[zz, yy])
                    if (n - 1) % 2 == m:
                        copies.append(copy_to(dst, dst, s_y.at[2, n - 1], r_own.at[zz, yy], tensor=wrap(y - step, NY)))
                        copies[-1].start()
                    to_sibling(zz, yy, dst)
            if n >= 2:
                zz = wrap(z + order[n - 2][0], NZ)
                yy = wrap(y + 2, NY)
                arrived(ublk(1, zz, yy), r_own.at[zz, yy])
                to_sibling(zz, yy, ublk(1, zz, yy))
        for copy in copies:
            copy.wait_send()

    def wait_sibling(n, carry):
        zz, yy = lax.div(n, NY), lax.rem(n, NY)
        arrived(ublk(1 - core, zz, yy), r_sib.at[zz, yy])
        return carry

    lax.fori_loop(0, NZ * NY, wait_sibling, 0)
    keep_own.wait()

    chunk = 512
    groups = chunk // 128

    def section_rows(k):
        return pl.ds(((k % 2) * NZ + k // 2) * tok, tok)

    SQ[...] = jnp.zeros_like(SQ)

    def squares(f, carry):
        cols = pl.ds(pl.multiple_of(f * chunk, chunk), chunk)
        hidden = jnp.zeros((tok, chunk), F32)
        for k in range(2 * NZ):
            hidden = hidden + U[section_rows(k), cols].astype(F32)
            square = hidden * hidden
            part = square[:, :128]
            for g in range(1, groups):
                part = part + square[:, g * 128:(g + 1) * 128]
            SQ[section_rows(k), :] += part
        return carry

    def gain_row(f, count):
        return jnp.concatenate([GAIN[pl.ds(f * count + g, 1), :] for g in range(count)], axis=1)

    GAIN[...] = gain[...].astype(F32)
    lax.fori_loop(0, width // chunk, squares, 0)
    mean = jnp.sum(SQ[...], axis=1, keepdims=True) / width
    INV[...] = jnp.broadcast_to(lax.rsqrt(mean + epsilon), (rows, 128))

    def normalize(f, carry):
        cols = pl.ds(pl.multiple_of(f * chunk, chunk), chunk)
        scale = gain_row(f, groups)
        hidden = jnp.zeros((tok, chunk), F32)
        for k in range(2 * NZ):
            hidden = hidden + U[section_rows(k), cols].astype(F32)
            inverse = INV[section_rows(k), :]
            R[section_rows(k), cols] = (
                scale * hidden * jnp.concatenate([inverse] * groups, axis=1)
            ).astype(BF16)
        return carry

    lax.fori_loop(0, width // chunk, normalize, 0)

    part = width // NX

    def slice_x(xx):
        return pl.ds(pl.multiple_of(xx * part, part), part)

    def rx_rows(xx, cc):
        return pl.ds(pl.multiple_of(xx * rows + cc * half, half), half)

    def x_rows(xx):
        return pl.ds(pl.multiple_of(xx * rows, rows), rows)

    row_copies = []
    for n, d in enumerate((1, -1, 2)):
        xx = wrap(x + d, NX)
        row_copies.append(copy_to(
            R.at[half_rows(core), slice_x(xx)], RX.at[rx_rows(x, core), :],
            s_rx.at[n], r_rx.at[x], dp=xx,
        ))
        row_copies[-1].start()
    keep_rows = pltpu.make_async_copy(R.at[:, slice_x(x)], RX.at[x_rows(x), :], local_sem.at[3])
    keep_rows.start()

    load_head.wait()
    depth = 1024
    pad = lax.broadcasted_iota(jnp.int32, (vpad, rows), 0) >= vdev
    L[...] = jnp.where(pad, -1e30, 0.0)

    def logits_step(f, carry):
        cols = pl.ds(pl.multiple_of(f * depth, depth), depth)
        L[0:vdev, :] += lax.dot_general(
            H[:, cols], R[:, cols], (((1,), (1,)), ((), ())), preferred_element_type=F32
        )
        return carry

    lax.fori_loop(0, width // depth, logits_step, 0)

    first = (s * NY + y) * vdev
    column = lax.broadcasted_iota(jnp.int32, (1, rows), 1)
    token = lax.rem(column, tok)
    block = lax.div(column, tok)
    wanted = jnp.zeros((1, rows), jnp.int32)
    for i in range(tok):
        wanted = jnp.where(token == i, targets[i], wanted)
    numerator = jnp.zeros((1, rows), jnp.int32)
    for b in range(2 * NZ):
        numerator = jnp.where(block == b, curriculum[(b % NZ) * 2 + b // NZ], numerator)
    weight = numerator.astype(F32) / scale_denominator
    hit = lax.broadcasted_iota(jnp.int32, (vpad, rows), 0) + first == wanted
    hit = jnp.logical_and(hit, jnp.logical_not(pad))
    logits = L[...]
    top = jnp.max(logits, axis=0, keepdims=True)
    total = jnp.sum(jnp.exp(logits - top), axis=0, keepdims=True)
    target = jnp.sum(jnp.where(hit, logits, 0.0), axis=0, keepdims=True)
    ST1[core] = jnp.concatenate([top, total, target, jnp.zeros((5, rows), F32)], axis=0)

    def combine(parts):
        top = parts[0][0:1]
        for p in parts[1:]:
            top = jnp.maximum(top, p[0:1])
        total = parts[0][1:2] * jnp.exp(parts[0][0:1] - top)
        target = parts[0][2:3]
        for p in parts[1:]:
            total = total + p[1:2] * jnp.exp(p[0:1] - top)
            target = target + p[2:3]
        return jnp.concatenate([top, total, target, jnp.zeros((5, rows), F32)], axis=0)

    def add_up(parts):
        total = parts[0]
        for p in parts[1:]:
            total = total + p
        return total

    def exchange(level, B1, B2, B3, ssem, r1, r2, r3):
        if level == 1:
            out = [copy_to(B1.at[core], B1.at[core], ssem.at[0], r1.at[core], section=sibling)]
        elif level == 2:
            out = [
                copy_to(B2.at[y], B2.at[y], ssem.at[n + 1], r2.at[y], tensor=wrap(y + d, NY))
                for n, d in enumerate((2, 1, 3))
            ]
        else:
            out = [
                copy_to(B3.at[z], B3.at[z], ssem.at[n + NY], r3.at[z], section=at_z(z + d))
                for n, d in enumerate((4, 3, 5, 2, 6, 1, 7))
            ]
        for copy in out:
            copy.start()
        return out

    def collect(level, B1, B2, B3, r1, r2, r3):
        if level == 1:
            arrived(B1.at[1 - core], r1.at[1 - core])
            return [B1[k] for k in range(2)]
        if level == 2:
            for d in (1, 3, 2):
                arrived(B2.at[wrap(y + d, NY)], r2.at[wrap(y + d, NY)])
            return [B2[k] for k in range(NY)]
        for d in (1, 7, 2, 6, 3, 5, 4):
            arrived(B3.at[wrap(z + d, NZ)], r3.at[wrap(z + d, NZ)])
        return [B3[k] for k in range(NZ)]

    small = []
    stat_bufs, stat_sems = (ST1, ST2, ST3), (r_st1, r_st2, r_st3)
    small += exchange(1, *stat_bufs, s_st, *stat_sems)
    ST2[y] = combine(collect(1, *stat_bufs, *stat_sems))
    small += exchange(2, *stat_bufs, s_st, *stat_sems)
    ST3[z] = combine(collect(2, *stat_bufs, *stat_sems))
    small += exchange(3, *stat_bufs, s_st, *stat_sems)
    final = combine(collect(3, *stat_bufs, *stat_sems))
    lse_row = final[0:1] + jnp.log(final[1:2])
    NL[x] = jnp.broadcast_to(lse_row - final[2:3], (8, rows))
    for n, d in enumerate((1, 2, 3)):
        small.append(copy_to(NL.at[x], NL.at[x], s_nl.at[n], r_nl.at[x], dp=wrap(x + d, NX)))
        small[-1].start()

    logits = L[...]
    probs = jnp.exp(logits - lse_row)
    grad = weight * (probs - jnp.where(hit, 1.0, 0.0))
    rounded = grad.astype(BF16)
    GX[x] = rounded
    GN[...] = jnp.transpose(rounded)
    product = jnp.sum(rounded.astype(F32) * logits, axis=0, keepdims=True)
    CT1[core] = jnp.broadcast_to(product, (8, rows))
    inner_bufs, inner_sems = (CT1, CT2, CT3), (r_ct1, r_ct2, r_ct3)
    small += exchange(1, *inner_bufs, s_ct, *inner_sems)
    for n, d in enumerate((1, -1, 2)):
        row_copies.append(copy_to(
            GX.at[x], GX.at[x], s_g.at[n], r_g.at[x], dp=wrap(x + d, NX)
        ))
        row_copies[-1].start()

    sib_copies = []
    for j in range(NY):
        yy = wrap(y + SCATTER_Y[j], NY)

        def share(f, carry):
            cols = pl.ds(pl.multiple_of(yy * q + f * chunk, chunk), chunk)
            term = jnp.dot(GN[:, 0:vdev], H[:, cols], preferred_element_type=F32)
            later = jnp.zeros((tok, chunk), F32)
            for k in reversed(range(2 * NZ)):
                at = ((k % 2) * NZ + k // 2) * tok
                inverse = INV[section_rows(k), :]
                later = later + term[at:at + tok] * jnp.concatenate([inverse] * groups, axis=1)
                PB[section_rows(k), cols] = later
            return carry

        lax.fori_loop(0, q // chunk, share, 0)
        sib_copies.append(copy_to(
            PB.at[half_rows(1 - core), slice_y(yy)], SB.at[:, slice_y(yy)],
            s_sb.at[j], r_sb.at[j], section=sibling,
        ))
        sib_copies[-1].start()
        if j == 0:
            CT2[y] = add_up(collect(1, *inner_bufs, *inner_sems))
            small += exchange(2, *inner_bufs, s_ct, *inner_sems)
        if j == 2:
            CT3[z] = add_up(collect(2, *inner_bufs, *inner_sems))
            small += exchange(3, *inner_bufs, s_ct, *inner_sems)

    projected = add_up(collect(3, *inner_bufs, *inner_sems))[0:1]
    projected = jnp.transpose(jnp.broadcast_to(projected, (128, rows)))
    COEF[...] = INV[...] * INV[...] * projected / width

    def second_term(f, carry):
        cols = pl.ds(pl.multiple_of(y * q + f * chunk, chunk), chunk)
        hidden = jnp.zeros((tok, chunk), F32)
        later = jnp.zeros((tok, chunk), F32)
        for k in range(2 * NZ):
            hidden = hidden + U[section_rows(k), cols].astype(F32)
            factor = jnp.where(k >= s, COEF[section_rows(k), :], 0.0)
            later = later + hidden * jnp.concatenate([factor] * groups, axis=1)
        upd_grad[0, :, pl.ds(pl.multiple_of(f * chunk, chunk), chunk)] = later
        return carry

    lax.fori_loop(0, q // chunk, second_term, 0)
    own_gain = gain_row(y, q // 128)

    def held(cc, zz, yy):
        return PB.at[block_rows(cc, zz), slice_y(yy)]

    def pair_sum(cc, zz, yy):
        return PB[block_rows(cc, zz), slice_y(yy)] + SB[pl.ds(pl.multiple_of(zz * tok, tok), tok), slice_y(yy)]

    @pl.when(core == 0)
    def _():
        copies = []
        up = lambda o, j: o * NY + j
        down = lambda o, j: (NZ // 2 + o) * NY + j
        last = NZ * NY

        def ring(o, j, sign, slot):
            zz = wrap(z + sign * o, NZ)
            yy = wrap(y + SCATTER_Y[j], NY)
            total = pair_sum(0, zz, yy)
            first_half = (j < NY // 2) == (sign > 0)
            if o + 1 < NZ // 2 or (o + 1 == NZ // 2 and first_half):
                arrived(RB.at[slot(o, j)], r_rs.at[slot(o, j)])
                total = total + RB[slot(o, j)]
            PB[block_rows(0, zz), slice_y(yy)] = total
            copies.append(copy_to(
                held(0, zz, yy), RB.at[slot(o - 1, j)], s_rs.at[slot(o - 1, j)], r_rs.at[slot(o - 1, j)],
                section=at_z(z + sign),
            ))
            copies[-1].start()

        for o in range(NZ // 2, 0, -1):
            for j in range(NY):
                if o == NZ // 2:
                    arrived(SB.at[:, slice_y(wrap(y + SCATTER_Y[j], NY))], r_sb.at[j])
                if o < NZ // 2 or j < NY // 2:
                    ring(o, j, 1, up)
                if o < NZ // 2 or j >= NY // 2:
                    ring(o, j, -1, down)
        for j in range(NY):
            yy = wrap(y + SCATTER_Y[j], NY)
            arrived(RB.at[up(0, j)], r_rs.at[up(0, j)])
            arrived(RB.at[down(0, j)], r_rs.at[down(0, j)])
            total = pair_sum(0, z, yy) + RB[up(0, j)] + RB[down(0, j)]
            if j < NY - 1:
                PB[block_rows(0, z), slice_y(yy)] = total
                copies.append(copy_to(
                    held(0, z, yy), RB.at[last + j], s_rs.at[last + j], r_rs.at[last + j], tensor=yy
                ))
                copies[-1].start()
        for j in (1, 2, 0):
            arrived(RB.at[last + j], r_rs.at[last + j])
            total = total + RB[last + j]
        upd_grad[0] = own_gain * total - upd_grad[0]
        for copy in copies:
            copy.wait_send()

    @pl.when(core == 1)
    def _():
        copies = []
        count = len(SCATTER_Z)
        far, plus, minus = 0, count, 2 * count
        zplus, zminus = 3 * count, 3 * count + NZ // 2

        def send(src, slot, **device):
            copies.append(copy_to(src, RB.at[slot], s_rs.at[slot], r_rs.at[slot], **device))
            copies[-1].start()

        for j in range(NY):
            yy = wrap(y + SCATTER_Y[j], NY)
            arrived(SB.at[:, slice_y(yy)], r_sb.at[j])
            for n in range(count):
                zz = wrap(z + SCATTER_Z[n], NZ)
                total = pair_sum(1, zz, yy)
                if j == 0:
                    PB[block_rows(1, zz), slice_y(yy)] = total
                    send(held(1, zz, yy), far + n, tensor=wrap(y + (1 if n % 2 == 0 else -1), NY))
                elif j < NY - 1:
                    step = SCATTER_Y[j]
                    if (n % 2 == 0) == (step == 1):
                        arrived(RB.at[far + n], r_rs.at[far + n])
                        total = total + RB[far + n]
                    PB[block_rows(1, zz), slice_y(yy)] = total
                    send(held(1, zz, yy), (plus if step == 1 else minus) + n, tensor=yy)
                else:
                    arrived(RB.at[plus + n], r_rs.at[plus + n])
                    arrived(RB.at[minus + n], r_rs.at[minus + n])
                    total = total + RB[plus + n] + RB[minus + n]
                    o = SCATTER_Z[n]
                    if o == 0:
                        arrived(RB.at[zplus], r_rs.at[zplus])
                        arrived(RB.at[zminus], r_rs.at[zminus])
                        total = total + RB[zplus] + RB[zminus]
                        upd_grad[0] = own_gain * total - upd_grad[0]
                    else:
                        base, sign = (zplus, 1) if o > 0 else (zminus, -1)
                        depth_here = abs(o)
                        if depth_here < (NZ // 2 if o > 0 else NZ // 2 - 1):
                            arrived(RB.at[base + depth_here], r_rs.at[base + depth_here])
                            total = total + RB[base + depth_here]
                        PB[block_rows(1, zz), slice_y(yy)] = total
                        send(held(1, zz, yy), base + depth_here - 1, section=at_z(z + sign))
        for copy in copies:
            copy.wait_send()

    keep_rows.wait()
    for d in (1, -1, 2):
        xx = wrap(x + d, NX)
        dst = RX.at[rx_rows(xx, core), :]
        arrived(dst, r_rx.at[xx])
        row_copies.append(copy_to(dst, dst, s_rxs.at[xx], r_rxs.at[xx], section=sibling))
        row_copies[-1].start()
    for d in (1, -1, 2):
        xx = wrap(x + d, NX)
        arrived(GX.at[xx], r_g.at[xx])
        arrived(RX.at[rx_rows(xx, 1 - core), :], r_rxs.at[xx])
        arrived(NL.at[xx], r_nl.at[xx])

    def head_part(f, carry):
        cols = pl.ds(pl.multiple_of(f * 256, 256), 256)
        total = jnp.zeros((vpad, 256), F32)
        for k in range(NX):
            total = total + jnp.dot(GX[k], RX[k * rows:(k + 1) * rows, cols], preferred_element_type=F32)
        head_grad[:, cols] = total[0:vdev].astype(BF16)
        return carry

    lax.fori_loop(0, part // 256, head_part, 0)

    nll = add_up([NL[k] for k in range(NX)])
    nll = jnp.transpose(jnp.broadcast_to(nll[0:1], (128, rows)))
    for b in range(2 * NZ):
        section = (b % NZ) * 2 + b // NZ
        losses[section:section + 1, :] = jnp.sum(
            nll[b * tok:(b + 1) * tok], axis=0, keepdims=True
        ) / (tok * NX)

    for copy in row_copies + sib_copies + small:
        copy.wait_send()


def body(updates, norm_gain, head, targets, curriculum):
    _, tok, q = updates.shape
    width, vdev = head.shape
    vpad = (vdev + 15) // 16 * 16
    rows = 2 * NZ * tok
    vmem = pl.BlockSpec(memory_space=pltpu.VMEM)
    smem = pl.BlockSpec(memory_space=pltpu.SMEM)
    dma = lambda *shape: pltpu.SemaphoreType.DMA(shape)
    slots = NZ * NY + NY
    upd_grad, head_grad, losses = pl.pallas_call(
        kernel,
        out_shape=(
            jax.ShapeDtypeStruct((1, tok, q), F32),
            jax.ShapeDtypeStruct((vdev, width // NX), BF16),
            jax.ShapeDtypeStruct((2 * NZ, 128), F32),
        ),
        in_specs=[vmem, vmem, pl.BlockSpec(memory_space=pl.ANY), smem, smem],
        out_specs=(vmem, vmem, vmem),
        scratch_shapes=[
            pltpu.VMEM((rows, width), BF16),
            pltpu.VMEM((vdev, width), BF16),
            pltpu.VMEM((rows, width), BF16),
            pltpu.VMEM((rows, width), F32),
            pltpu.VMEM((rows // 2, width), F32),
            pltpu.VMEM((slots, tok, q), F32),
            pltpu.VMEM((NX * rows, width // NX), BF16),
            pltpu.VMEM((NX, vpad, rows), BF16),
            pltpu.VMEM((rows, vpad), BF16),
            pltpu.VMEM((vpad, rows), F32),
            pltpu.VMEM((width // 128, 128), F32),
            pltpu.VMEM((rows, 128), F32),
            pltpu.VMEM((rows, 128), F32),
            pltpu.VMEM((rows, 128), F32),
            pltpu.VMEM((2, 8, rows), F32),
            pltpu.VMEM((NY, 8, rows), F32),
            pltpu.VMEM((NZ, 8, rows), F32),
            pltpu.VMEM((2, 8, rows), F32),
            pltpu.VMEM((NY, 8, rows), F32),
            pltpu.VMEM((NZ, 8, rows), F32),
            pltpu.VMEM((NX, 8, rows), F32),
            dma(4), dma(NZ, NY), dma(NZ, NY), dma(NZ, NY), dma(NZ, NY), dma(NZ, NY), dma(3, NZ),
            dma(NY + NZ), dma(2), dma(NY), dma(NZ), dma(NY + NZ), dma(2), dma(NY), dma(NZ), dma(NX), dma(NX),
            dma(NX), dma(NX), dma(NX), dma(NX), dma(NX), dma(NX), dma(NY), dma(NY), dma(slots), dma(slots),
        ],
        compiler_params=pltpu.CompilerParams(
            collective_id=0, has_side_effects=True, vmem_limit_bytes=60 * 1024 * 1024
        ),
    )(updates, norm_gain.reshape(width // 128, 128), head.T, targets, curriculum)
    return upd_grad, head_grad.T, losses[:, 0]


def solution(mesh):
    return jax.shard_map(
        body,
        mesh=mesh,
        in_specs=(P("section", "dp", "tensor"), P(), P(None, ("section", "tensor")), P("dp"), P()),
        out_specs=(P("section", "dp", "tensor"), P("dp", ("section", "tensor")), P()),
        check_vma=False,
    )
```

```python
import jax
import jax.numpy as jnp
from jax import lax
from jax.experimental import pallas as pl
from jax.experimental.pallas import tpu as pltpu
from jax.sharding import PartitionSpec as P

F32 = jnp.float32
BF16 = jnp.bfloat16
epsilon = 1e-05
scale_denominator = 4.0

NY = 4
NX = 4
NZ = 8

GATHER_Y = (0, -1, 1, 2)
SCATTER_Y = (2, 1, -1, 0)
SCATTER_Z = (4, 3, -3, 2, -2, 1, -1, 0)


def wrap(value, count):
    return lax.rem(value + 2 * count, count)


CODE_TOP = 32766.0


def encode(value):
    root = value * lax.rsqrt(jnp.maximum(jnp.abs(value), 1e-12))
    return jnp.round(root).astype(jnp.int32).astype(jnp.int16)


def decode(code):
    root = code.astype(jnp.int32).astype(F32)
    return root * jnp.abs(root)


def kernel(
    upd, gain, head, targets, curriculum,
    upd_grad, head_grad, losses,
    U, H, R, PB, QS, SB, QR, RB, RX, GX, GN, L, GAIN, SQ, INV, COEF, BND, SC, HG, ST1, ST2, CT1, CT2, NL,
    local_sem, r_own, r_sib, s_sib, s_p, s_m, s_y,
    s_st, r_st1, r_st2, s_ct, r_ct1, r_ct2, s_nl, r_nl, s_hg,
    s_rx, r_rx, s_rxs, r_rxs, s_g, r_g, s_sb, r_sb, s_rs, r_rs,
):
    tok, q = upd.shape[1], upd.shape[2]
    width = q * NY
    vdev = head.shape[0]
    vpad = L.shape[0]
    half = NZ * tok
    rows = 2 * half
    s = lax.axis_index("section")
    y = lax.axis_index("tensor")
    x = lax.axis_index("dp")
    core = lax.rem(s, 2)
    z = lax.div(s, 2)
    sibling = s + 1 - 2 * core

    def copy_to(src, dst, ssem, rsem, **device):
        return pltpu.make_async_remote_copy(
            src_ref=src, dst_ref=dst, send_sem=ssem, recv_sem=rsem,
            device_id=device, device_id_type=pl.DeviceIdType.MESH,
        )

    def arrived(dst, rsem):
        copy_to(dst, dst, local_sem.at[0], rsem, section=sibling).wait_recv()

    def at_z(zz):
        return 2 * wrap(zz, NZ) + core

    def block_rows(cc, zz):
        return pl.ds(pl.multiple_of((cc * NZ + zz) * tok, tok), tok)

    def slice_y(yy):
        return pl.ds(pl.multiple_of(yy * q, q), q)

    def half_rows(cc):
        return pl.ds(pl.multiple_of(cc * half, half), half)

    barrier = pltpu.get_barrier_semaphore()
    peers = [dict(section=sibling)]
    peers += [dict(tensor=wrap(y + d, NY)) for d in range(1, NY)]
    peers += [dict(section=sibling, tensor=wrap(y + d, NY)) for d in range(1, NY)]
    peers += [dict(section=at_z(z + d)) for d in range(1, NZ)]
    peers += [dict(dp=wrap(x + d, NX)) for d in range(1, NX)]
    for peer in peers:
        pl.semaphore_signal(barrier, inc=1, device_id=peer, device_id_type=pl.DeviceIdType.MESH)
    load_head = pltpu.make_async_copy(head, H, local_sem.at[1])
    load_head.start()
    pl.semaphore_wait(barrier, len(peers))

    own = upd.at[0]

    def ublk(cc, zz, yy):
        return U.at[block_rows(cc, zz), slice_y(yy)]

    keep_own = pltpu.make_async_copy(own, ublk(core, z, y), local_sem.at[2])
    keep_own.start()

    @pl.when(core == 0)
    def _():
        copies = []

        def pass_on(src, zz, yy, k, j):
            dst = ublk(0, zz, yy)
            near = k + 1 < NZ // 2
            if k >= 0 and (near or (k + 1 == NZ // 2 and j < NY // 2)) and src[1] != "right":
                copies.append(copy_to(src[0], dst, s_p.at[k, j], r_own.at[zz, yy], section=at_z(z + 1)))
                copies[-1].start()
            if k >= 0 and (near or (k + 1 == NZ // 2 and j >= NY // 2)) and src[1] != "left":
                copies.append(copy_to(src[0], dst, s_m.at[k, j], r_own.at[zz, yy], section=at_z(z - 1)))
                copies[-1].start()
            copies.append(copy_to(src[0], dst, s_sib.at[zz, yy], r_sib.at[zz, yy], section=sibling))
            copies[-1].start()

        for n, d in enumerate((1, -1, 2)):
            copies.append(copy_to(own, ublk(0, z, y), s_y.at[n, 0], r_own.at[z, y], tensor=wrap(y + d, NY)))
            copies[-1].start()
        pass_on((own, "here"), z, y, 0, 0)
        for j in range(1, NY):
            yy = wrap(y + GATHER_Y[j], NY)
            arrived(ublk(0, z, yy), r_own.at[z, yy])
            pass_on((ublk(0, z, yy), "here"), z, yy, 0, j)
        for k in range(1, NZ // 2 + 1):
            for j in range(NY):
                yy = wrap(y + GATHER_Y[j], NY)
                if k < NZ // 2 or j < NY // 2:
                    zz = wrap(z - k, NZ)
                    arrived(ublk(0, zz, yy), r_own.at[zz, yy])
                    pass_on((ublk(0, zz, yy), "left"), zz, yy, k, j)
                if k < NZ // 2 or j >= NY // 2:
                    zz = wrap(z + k, NZ)
                    arrived(ublk(0, zz, yy), r_own.at[zz, yy])
                    pass_on((ublk(0, zz, yy), "right"), zz, yy, k, j)
        for copy in copies:
            copy.wait_send()

    @pl.when(core == 1)
    def _():
        copies = []
        order = (0, -1, 1, -2, 2, -3, 3, -4)

        def send(src, dst, ssem, rsem, **device):
            copies.append(copy_to(src, dst, ssem, rsem, **device))
            copies[-1].start()

        for n, d in enumerate(order):
            zz = wrap(z + d, NZ)
            dst = ublk(1, zz, y)
            src = own if n == 0 else dst
            if n > 0:
                arrived(dst, r_own.at[zz, y])
            if d in (0, -2):
                send(src, dst, s_p.at[-d, 0], r_own.at[zz, y], section=at_z(z + 1))
                send(src, dst, s_p.at[-d, 1], r_own.at[zz, y], section=at_z(z + 2))
            if d in (0, 2):
                send(src, dst, s_m.at[d, 0], r_own.at[zz, y], section=at_z(z - 1))
            if d == 0:
                send(src, dst, s_m.at[d, 1], r_own.at[zz, y], section=at_z(z - 2))
            for m, step in enumerate((1, -1, 2)):
                send(src, dst, s_y.at[m, n], r_own.at[zz, y], tensor=wrap(y + step, NY))
            send(src, dst, s_sib.at[zz, y], r_sib.at[zz, y], section=sibling)
        for d in order:
            zz = wrap(z + d, NZ)
            for step in (-1, 1, 2):
                yy = wrap(y + step, NY)
                dst = ublk(1, zz, yy)
                arrived(dst, r_own.at[zz, yy])
                send(dst, dst, s_sib.at[zz, yy], r_sib.at[zz, yy], section=sibling)
        for copy in copies:
            copy.wait_send()

    load_head.wait()

    def largest(f, carry):
        cols = pl.ds(pl.multiple_of(f * 256, 256), 256)
        value = jnp.max(jnp.abs(H[:, cols]).astype(F32), axis=0, keepdims=True)
        return jnp.maximum(carry, value)

    head_top = lax.fori_loop(0, width // 256, largest, jnp.zeros((1, 256), F32))
    head_top = jnp.max(head_top, axis=1, keepdims=True)

    def wait_sibling(n, carry):
        zz, yy = lax.div(n, NY), lax.rem(n, NY)
        arrived(ublk(1 - core, zz, yy), r_sib.at[zz, yy])
        return carry

    lax.fori_loop(0, NZ * NY, wait_sibling, 0)
    keep_own.wait()

    chunk = 512
    groups = chunk // 128

    def section_rows(k):
        return pl.ds(((k % 2) * NZ + k // 2) * tok, tok)

    SQ[...] = jnp.zeros_like(SQ)

    def squares(f, carry):
        cols = pl.ds(pl.multiple_of(f * chunk, chunk), chunk)
        hidden = jnp.zeros((tok, chunk), F32)
        for k in range(2 * NZ):
            hidden = hidden + U[section_rows(k), cols].astype(F32)
            square = hidden * hidden
            part = square[:, :128]
            for g in range(1, groups):
                part = part + square[:, g * 128:(g + 1) * 128]
            SQ[section_rows(k), :] += part
        return carry

    def gain_row(f, count):
        return jnp.concatenate([GAIN[pl.ds(f * count + g, 1), :] for g in range(count)], axis=1)

    GAIN[...] = gain[...].astype(F32)
    lax.fori_loop(0, width // chunk, squares, 0)
    mean = jnp.sum(SQ[...], axis=1, keepdims=True) / width
    INV[...] = jnp.broadcast_to(lax.rsqrt(mean + epsilon), (rows, 128))

    def normalize(f, carry):
        cols = pl.ds(pl.multiple_of(f * chunk, chunk), chunk)
        scale = gain_row(f, groups)
        hidden = jnp.zeros((tok, chunk), F32)
        for k in range(2 * NZ):
            hidden = hidden + U[section_rows(k), cols].astype(F32)
            inverse = INV[section_rows(k), :]
            R[section_rows(k), cols] = (
                scale * hidden * jnp.concatenate([inverse] * groups, axis=1)
            ).astype(BF16)
        return carry

    lax.fori_loop(0, width // chunk, normalize, 0)

    part = width // NX

    def slice_x(xx):
        return pl.ds(pl.multiple_of(xx * part, part), part)

    def rx_rows(xx, cc):
        return pl.ds(pl.multiple_of(xx * rows + cc * half, half), half)

    def x_rows(xx):
        return pl.ds(pl.multiple_of(xx * rows, rows), rows)

    row_copies = []
    for n, d in enumerate((1, -1, 2)):
        xx = wrap(x + d, NX)
        row_copies.append(copy_to(
            R.at[half_rows(core), slice_x(xx)], RX.at[rx_rows(x, core), :],
            s_rx.at[n], r_rx.at[x], dp=xx,
        ))
        row_copies[-1].start()
    keep_rows = pltpu.make_async_copy(R.at[:, slice_x(x)], RX.at[x_rows(x), :], local_sem.at[3])
    keep_rows.start()

    depth = 2048
    pad = lax.broadcasted_iota(jnp.int32, (vpad, rows), 0) >= vdev
    L[...] = jnp.where(pad, -1e30, 0.0)

    def logits_step(f, carry):
        cols = pl.ds(pl.multiple_of(f * depth, depth), depth)
        L[0:vdev, :] += lax.dot_general(
            H[:, cols], R[:, cols], (((1,), (1,)), ((), ())), preferred_element_type=F32
        )
        return carry

    lax.fori_loop(0, width // depth, logits_step, 0)

    first = (s * NY + y) * vdev
    column = lax.broadcasted_iota(jnp.int32, (1, rows), 1)
    token = lax.rem(column, tok)
    block = lax.div(column, tok)
    wanted = jnp.zeros((1, rows), jnp.int32)
    for i in range(tok):
        wanted = jnp.where(token == i, targets[i], wanted)
    numerator = jnp.zeros((1, rows), jnp.int32)
    for b in range(2 * NZ):
        numerator = jnp.where(block == b, curriculum[(b % NZ) * 2 + b // NZ], numerator)
    weight = numerator.astype(F32) / scale_denominator
    hit = lax.broadcasted_iota(jnp.int32, (vpad, rows), 0) + first == wanted
    hit = jnp.logical_and(hit, jnp.logical_not(pad))
    logits = L[...]
    top = jnp.max(logits, axis=0, keepdims=True)
    total = jnp.sum(jnp.exp(logits - top), axis=0, keepdims=True)
    target = jnp.sum(jnp.where(hit, logits, 0.0), axis=0, keepdims=True)
    here = core * NY + y
    ST1[here] = jnp.concatenate(
        [top, total, target, jnp.broadcast_to(head_top, (1, rows)), jnp.zeros((4, rows), F32)], axis=0
    )

    def combine(parts):
        top = parts[0][0:1]
        for p in parts[1:]:
            top = jnp.maximum(top, p[0:1])
        total = parts[0][1:2] * jnp.exp(parts[0][0:1] - top)
        target = parts[0][2:3]
        largest = parts[0][3:4]
        for p in parts[1:]:
            largest = jnp.maximum(largest, p[3:4])
            total = total + p[1:2] * jnp.exp(p[0:1] - top)
            target = target + p[2:3]
        return jnp.concatenate([top, total, target, largest, jnp.zeros((4, rows), F32)], axis=0)

    def add_up(parts):
        total = parts[0]
        for p in parts[1:]:
            total = total + p
        return total

    def exchange(level, B1, B2, ssem, r1, r2):
        if level == 1:
            out = [copy_to(B1.at[here], B1.at[here], ssem.at[0], r1.at[here], section=sibling)]
            for n, d in enumerate((1, 3, 2)):
                yy = wrap(y + d, NY)
                out.append(copy_to(B1.at[here], B1.at[here], ssem.at[n + 1], r1.at[here], tensor=yy))
                out.append(copy_to(
                    B1.at[here], B1.at[here], ssem.at[n + NY], r1.at[here], section=sibling, tensor=yy
                ))
        else:
            out = [
                copy_to(B2.at[z], B2.at[z], ssem.at[n + 2 * NY], r2.at[z], section=at_z(z + d))
                for n, d in enumerate((4, 3, 5, 2, 6, 1, 7))
            ]
        for copy in out:
            copy.start()
        return out

    def collect(level, B1, B2, r1, r2):
        if level == 1:
            for cc, d in ((1, 0), (0, 1), (0, 3), (1, 1), (1, 3), (0, 2), (1, 2)):
                slot = lax.rem(core + cc, 2) * NY + wrap(y + d, NY)
                arrived(B1.at[slot], r1.at[slot])
            return [B1[k] for k in range(2 * NY)]
        for d in (1, 7, 2, 6, 3, 5, 4):
            arrived(B2.at[wrap(z + d, NZ)], r2.at[wrap(z + d, NZ)])
        return [B2[k] for k in range(NZ)]

    small = []
    stat_bufs, stat_sems = (ST1, ST2), (r_st1, r_st2)
    small += exchange(1, *stat_bufs, s_st, *stat_sems)
    ST2[z] = combine(collect(1, *stat_bufs, *stat_sems))
    small += exchange(2, *stat_bufs, s_st, *stat_sems)
    final = combine(collect(2, *stat_bufs, *stat_sems))
    lse_row = final[0:1] + jnp.log(final[1:2])
    NL[x] = jnp.broadcast_to(lse_row - final[2:3], (8, rows))
    for n, d in enumerate((1, 2, 3)):
        small.append(copy_to(NL.at[x], NL.at[x], s_nl.at[n], r_nl.at[x], dp=wrap(x + d, NX)))
        small[-1].start()

    logits = L[...]
    probs = jnp.exp(logits - lse_row)
    grad = weight * (probs - jnp.where(hit, 1.0, 0.0))
    rounded = grad.astype(BF16)
    GX[x] = rounded
    GN[...] = jnp.transpose(rounded)
    product = jnp.sum(rounded.astype(F32) * logits, axis=0, keepdims=True)
    CT1[here] = jnp.broadcast_to(product, (8, rows))
    inner_bufs, inner_sems = (CT1, CT2), (r_ct1, r_ct2)
    small += exchange(1, *inner_bufs, s_ct, *inner_sems)
    for n, d in enumerate((1, -1, 2)):
        row_copies.append(copy_to(
            GX.at[x], GX.at[x], s_g.at[n], r_g.at[x], dp=wrap(x + d, NX)
        ))
        row_copies[-1].start()

    later = jnp.zeros((tok, 128), F32)
    for k in reversed(range(2 * NZ)):
        later = later + INV[section_rows(k), :] * (curriculum[k].astype(F32) / scale_denominator)
        bound = jnp.maximum(later * (final[3:4, 0:128] * 2.03), 1e-20)
        BND[section_rows(k), :] = bound
        SC[section_rows(k), :] = (CODE_TOP * CODE_TOP) / bound

    sib_copies = []
    for j in range(NY):
        yy = wrap(y + SCATTER_Y[j], NY)

        def share(f, carry):
            cols = pl.ds(pl.multiple_of(yy * q + f * chunk, chunk), chunk)
            term = jnp.dot(GN[:, 0:vdev], H[:, cols], preferred_element_type=F32)
            later = jnp.zeros((tok, chunk), F32)
            for k in reversed(range(2 * NZ)):
                at = ((k % 2) * NZ + k // 2) * tok
                inverse = INV[section_rows(k), :]
                later = later + term[at:at + tok] * jnp.concatenate([inverse] * groups, axis=1)
                PB[section_rows(k), cols] = later * jnp.concatenate([SC[section_rows(k), :]] * groups, axis=1)
            QS[:, cols] = encode(PB[half_rows(1 - core), cols])
            return carry

        lax.fori_loop(0, q // chunk, share, 0)
        sib_copies.append(copy_to(
            QS.at[:, slice_y(yy)], SB.at[:, slice_y(yy)],
            s_sb.at[j], r_sb.at[j], section=sibling,
        ))
        sib_copies[-1].start()
        if j == 1:
            CT2[z] = add_up(collect(1, *inner_bufs, *inner_sems))
            small += exchange(2, *inner_bufs, s_ct, *inner_sems)

    projected = add_up(collect(2, *inner_bufs, *inner_sems))[0:1]
    projected = jnp.transpose(jnp.broadcast_to(projected, (128, rows)))
    COEF[...] = INV[...] * INV[...] * projected / width

    def second_term(f, carry):
        cols = pl.ds(pl.multiple_of(y * q + f * chunk, chunk), chunk)
        hidden = jnp.zeros((tok, chunk), F32)
        later = jnp.zeros((tok, chunk), F32)
        for k in range(2 * NZ):
            hidden = hidden + U[section_rows(k), cols].astype(F32)
            factor = jnp.where(k >= s, COEF[section_rows(k), :], 0.0)
            later = later + hidden * jnp.concatenate([factor] * groups, axis=1)
        upd_grad[0, :, pl.ds(pl.multiple_of(f * chunk, chunk), chunk)] = later
        return carry

    lax.fori_loop(0, q // chunk, second_term, 0)
    own_gain = gain_row(y, q // 128)

    def pair_sum(cc, zz, yy):
        return PB[block_rows(cc, zz), slice_y(yy)] + decode(
            SB[pl.ds(pl.multiple_of(zz * tok, tok), tok), slice_y(yy)]
        )

    def pass_rows(copies, d):
        xx = wrap(x + d, NX)
        dst = RX.at[rx_rows(xx, core), :]
        arrived(dst, r_rx.at[xx])
        copies.append(copy_to(dst, dst, s_rxs.at[xx], r_rxs.at[xx], section=sibling))
        copies[-1].start()

    def rows_here():
        for d in (1, -1, 2):
            xx = wrap(x + d, NX)
            arrived(GX.at[xx], r_g.at[xx])
            arrived(RX.at[rx_rows(xx, 1 - core), :], r_rxs.at[xx])

    piece = part // (2 * NX)

    def head_part(f):
        cols = slice(f * piece, (f + 1) * piece)
        total = jnp.zeros((vpad, piece), F32)
        for k in range(NX):
            total = total + jnp.dot(GX[k], RX[k * rows:(k + 1) * rows, cols], preferred_element_type=F32)
        HG[:, cols] = total[0:vdev].astype(BF16)
        out = pltpu.make_async_copy(HG.at[:, cols], head_grad.at[:, cols], s_hg.at[f])
        out.start()
        return out

    keep_rows.wait()

    def write_update(total):
        back = BND[block_rows(core, z), :] / (CODE_TOP * CODE_TOP)
        total = total * jnp.concatenate([back] * (q // 128), axis=1)
        upd_grad[0] = own_gain * total - upd_grad[0]

    @pl.when(core == 0)
    def _():
        copies, outs = [], []
        up = lambda o, j: o * NY + j
        down = lambda o, j: (NZ // 2 + o) * NY + j
        last = NZ * NY

        def ring(o, j, sign, slot):
            zz = wrap(z + sign * o, NZ)
            yy = wrap(y + SCATTER_Y[j], NY)
            total = pair_sum(0, zz, yy)
            first_half = (j < NY // 2) == (sign > 0)
            if o + 1 < NZ // 2 or (o + 1 == NZ // 2 and first_half):
                arrived(RB.at[slot(o, j)], r_rs.at[slot(o, j)])
                total = total + decode(RB[slot(o, j)])
            QR[slot(o - 1, j)] = encode(total)
            copies.append(copy_to(
                QR.at[slot(o - 1, j)], RB.at[slot(o - 1, j)], s_rs.at[slot(o - 1, j)], r_rs.at[slot(o - 1, j)],
                section=at_z(z + sign),
            ))
            copies[-1].start()

        for o in range(NZ // 2, 0, -1):
            for j in range(NY):
                if o == NZ // 2:
                    arrived(SB.at[:, slice_y(wrap(y + SCATTER_Y[j], NY))], r_sb.at[j])
                if o < NZ // 2 or j < NY // 2:
                    ring(o, j, 1, up)
                if o < NZ // 2 or j >= NY // 2:
                    ring(o, j, -1, down)
                if o == 1:
                    outs += [head_part(2 * j), head_part(2 * j + 1)]
            if o == 3:
                pass_rows(copies, 1)
                pass_rows(copies, -1)
            if o == 2:
                pass_rows(copies, 2)
                rows_here()
        for j in range(NY):
            yy = wrap(y + SCATTER_Y[j], NY)
            arrived(RB.at[up(0, j)], r_rs.at[up(0, j)])
            arrived(RB.at[down(0, j)], r_rs.at[down(0, j)])
            total = pair_sum(0, z, yy) + decode(RB[up(0, j)]) + decode(RB[down(0, j)])
            if j < NY - 1:
                QR[last + j] = encode(total)
                copies.append(copy_to(
                    QR.at[last + j], RB.at[last + j], s_rs.at[last + j], r_rs.at[last + j], tensor=yy
                ))
                copies[-1].start()
        for j in (1, 2, 0):
            arrived(RB.at[last + j], r_rs.at[last + j])
            total = total + decode(RB[last + j])
        write_update(total)
        for copy in copies:
            copy.wait_send()
        for copy in outs:
            copy.wait()

    @pl.when(core == 1)
    def _():
        copies, outs = [], []
        count = len(SCATTER_Z)
        fourth, third, second, next_up, third_down, second_down, next_down = range(3 * count, 3 * count + 7)

        def send(value, slot, **device):
            QR[slot] = encode(value)
            copies.append(copy_to(QR.at[slot], RB.at[slot], s_rs.at[slot], r_rs.at[slot], **device))
            copies[-1].start()

        def received(slot):
            arrived(RB.at[slot], r_rs.at[slot])
            return decode(RB[slot])

        for j in range(NY - 1):
            yy = wrap(y + SCATTER_Y[j], NY)
            arrived(SB.at[:, slice_y(yy)], r_sb.at[j])
            for n in range(count):
                send(pair_sum(1, wrap(z + SCATTER_Z[n], NZ), yy), j * count + n, tensor=yy)
        pass_rows(copies, 1)
        pass_rows(copies, -1)
        arrived(SB.at[:, slice_y(y)], r_sb.at[NY - 1])
        for n, o in enumerate(SCATTER_Z):
            total = pair_sum(1, wrap(z + o, NZ), y)
            for j in range(NY - 1):
                total = total + received(j * count + n)
            if o == 4:
                send(total, fourth, section=at_z(z + 2))
            elif o == 3:
                send(total, third, section=at_z(z + 1))
            elif o == -3:
                send(total, third_down, section=at_z(z - 1))
            elif o == 2:
                send(total + received(fourth) + received(third), second, section=at_z(z + 2))
            elif o == -2:
                send(total + received(third_down), second_down, section=at_z(z - 2))
            elif o == 1:
                send(total, next_up, section=at_z(z + 1))
            elif o == -1:
                send(total, next_down, section=at_z(z - 1))
            if o == -2:
                pass_rows(copies, 2)
        rows_here()
        for n in range(count - 1):
            outs.append(head_part(n))
        for slot in (next_up, next_down, second, second_down):
            total = total + received(slot)
        write_update(total)
        outs.append(head_part(count - 1))
        for copy in copies:
            copy.wait_send()
        for copy in outs:
            copy.wait()

    for d in (1, -1, 2):
        xx = wrap(x + d, NX)
        arrived(NL.at[xx], r_nl.at[xx])
    nll = add_up([NL[k] for k in range(NX)])
    nll = jnp.transpose(jnp.broadcast_to(nll[0:1], (128, rows)))
    means = [None] * (2 * NZ)
    for b in range(2 * NZ):
        means[(b % NZ) * 2 + b // NZ] = jnp.sum(
            nll[b * tok:(b + 1) * tok], axis=0, keepdims=True
        ) / (tok * NX)
    means.append(jnp.zeros((128 - 2 * NZ, 128), F32))
    losses[...] = jnp.transpose(jnp.concatenate(means, axis=0))[0:8]

    for copy in row_copies + sib_copies + small:
        copy.wait_send()


def hand_over(upd_in, head_in, losses_in, upd_out, head_out, losses_out, upd_held, head_held, sem):
    count = 4
    step = head_in.shape[1] // count
    pairs = [(upd_in, upd_held, upd_out)]
    for n in range(count):
        cols = pl.ds(n * step, step)
        pairs.append((head_in.at[:, cols], head_held.at[:, cols], head_out.at[:, cols]))
    reads = [pltpu.make_async_copy(a, b, sem.at[0, n]) for n, (a, b, _) in enumerate(pairs)]
    writes = [pltpu.make_async_copy(b, c, sem.at[1, n]) for n, (_, b, c) in enumerate(pairs)]
    for copy in reads:
        copy.start()
    losses_out[...] = losses_in[0:1, 0:2 * NZ]
    for read, write in zip(reads, writes):
        read.wait()
        write.start()
    for copy in writes:
        copy.wait()


def body(updates, norm_gain, head, targets, curriculum):
    _, tok, q = updates.shape
    width, vdev = head.shape
    vpad = (vdev + 15) // 16 * 16
    rows = 2 * NZ * tok
    vmem = pl.BlockSpec(memory_space=pltpu.VMEM)
    smem = pl.BlockSpec(memory_space=pltpu.SMEM)
    hbm = pl.BlockSpec(memory_space=pl.ANY)
    dma = lambda *shape: pltpu.SemaphoreType.DMA(shape)
    slots = NZ * NY + NY
    upd_grad, head_grad, losses = pl.pallas_call(
        kernel,
        out_shape=(
            jax.ShapeDtypeStruct((1, tok, q), F32),
            jax.ShapeDtypeStruct((vdev, width // NX), BF16),
            jax.ShapeDtypeStruct((8, 128), F32),
        ),
        in_specs=[vmem, vmem, hbm, smem, smem],
        out_specs=(vmem, hbm, vmem),
        scratch_shapes=[
            pltpu.VMEM((rows, width), BF16),
            pltpu.VMEM((vdev, width), BF16),
            pltpu.VMEM((rows, width), BF16),
            pltpu.VMEM((rows, width), F32),
            pltpu.VMEM((rows // 2, width), jnp.int16),
            pltpu.VMEM((rows // 2, width), jnp.int16),
            pltpu.VMEM((slots, tok, q), jnp.int16),
            pltpu.VMEM((slots, tok, q), jnp.int16),
            pltpu.VMEM((NX * rows, width // NX), BF16),
            pltpu.VMEM((NX, vpad, rows), BF16),
            pltpu.VMEM((rows, vpad), BF16),
            pltpu.VMEM((vpad, rows), F32),
            pltpu.VMEM((width // 128, 128), F32),
            pltpu.VMEM((rows, 128), F32),
            pltpu.VMEM((rows, 128), F32),
            pltpu.VMEM((rows, 128), F32),
            pltpu.VMEM((rows, 128), F32),
            pltpu.VMEM((rows, 128), F32),
            pltpu.VMEM((vdev, width // NX), BF16),
            pltpu.VMEM((2 * NY, 8, rows), F32),
            pltpu.VMEM((NZ, 8, rows), F32),
            pltpu.VMEM((2 * NY, 8, rows), F32),
            pltpu.VMEM((NZ, 8, rows), F32),
            pltpu.VMEM((NX, 8, rows), F32),
            dma(4), dma(NZ, NY), dma(NZ, NY), dma(NZ, NY), dma(NZ, NY), dma(NZ, NY), dma(3, NZ),
            dma(2 * NY + NZ), dma(2 * NY), dma(NZ), dma(2 * NY + NZ), dma(2 * NY), dma(NZ), dma(NX), dma(NX), dma(NX * 2),
            dma(NX), dma(NX), dma(NX), dma(NX), dma(NX), dma(NX), dma(NY), dma(NY), dma(slots), dma(slots),
        ],
        compiler_params=pltpu.CompilerParams(
            collective_id=0, has_side_effects=True, vmem_limit_bytes=60 * 1024 * 1024
        ),
    )(updates, norm_gain.reshape(width // 128, 128), head.T, targets, curriculum)
    upd_grad, head_grad, losses = pl.pallas_call(
        hand_over,
        out_shape=(
            jax.ShapeDtypeStruct(upd_grad.shape, F32),
            jax.ShapeDtypeStruct(head_grad.shape, BF16),
            jax.ShapeDtypeStruct((1, 2 * NZ), F32),
        ),
        in_specs=[hbm, hbm, vmem],
        out_specs=(hbm, hbm, vmem),
        scratch_shapes=[pltpu.VMEM(upd_grad.shape, F32), pltpu.VMEM(head_grad.shape, BF16), dma(2, 5)],
        compiler_params=pltpu.CompilerParams(vmem_limit_bytes=60 * 1024 * 1024),
    )(upd_grad, head_grad, losses)
    return upd_grad, head_grad.T, losses.reshape(2 * NZ)


def solution(mesh):
    return jax.shard_map(
        body,
        mesh=mesh,
        in_specs=(P("section", "dp", "tensor"), P(), P(None, ("section", "tensor")), P("dp"), P()),
        out_specs=(P("section", "dp", "tensor"), P("dp", ("section", "tensor")), P()),
        check_vma=False,
    )
```

```python
import jax
import jax.numpy as jnp
from jax import lax
from jax.experimental import pallas as pl
from jax.experimental.pallas import tpu as pltpu
from jax.sharding import PartitionSpec as P

F32 = jnp.float32
BF16 = jnp.bfloat16
epsilon = 1e-05
scale_denominator = 4.0

NY = 4
NX = 4
NZ = 8

GATHER_Y = (0, -1, 1, 2)
SCATTER_Y = (2, 1, -1, 0)
SCATTER_Z = (4, 3, -3, 2, -2, 1, -1, 0)


def wrap(value, count):
    return lax.rem(value + 2 * count, count)


CODE_TOP = 32766.0


def encode(value):
    root = value * lax.rsqrt(jnp.maximum(jnp.abs(value), 1e-12))
    return jnp.round(root).astype(jnp.int32).astype(jnp.int16)


def decode(code):
    root = code.astype(jnp.int32).astype(F32)
    return root * jnp.abs(root)


def kernel(
    upd, gain, head, targets, curriculum,
    upd_grad, head_grad, losses,
    U, HEAD, H, HM, R, PB, QS, SB, QR, RB, RX, GX, GN, L, GAIN, SQ, INV, COEF, BND, SC, HG, ST1, ST2, CT1, CT2, NL,
    local_sem, r_own, r_sib, s_sib, s_p, s_m, s_y,
    s_st, r_st1, r_st2, s_ct, r_ct1, r_ct2, s_nl, r_nl, s_hg,
    s_rx, r_rx, s_rxs, r_rxs, s_g, r_g, s_sb, r_sb, s_rs, r_rs,
):
    tok, q = upd.shape[1], upd.shape[2]
    width = q * NY
    vdev = head.shape[0]
    vpad = L.shape[0]
    half = NZ * tok
    rows = 2 * half
    s = lax.axis_index("section")
    y = lax.axis_index("tensor")
    x = lax.axis_index("dp")
    core = lax.rem(s, 2)
    z = lax.div(s, 2)
    sibling = s + 1 - 2 * core

    def copy_to(src, dst, ssem, rsem, **device):
        return pltpu.make_async_remote_copy(
            src_ref=src, dst_ref=dst, send_sem=ssem, recv_sem=rsem,
            device_id=device, device_id_type=pl.DeviceIdType.MESH,
        )

    def arrived(dst, rsem):
        copy_to(dst, dst, local_sem.at[0], rsem, section=sibling).wait_recv()

    def at_z(zz):
        return 2 * wrap(zz, NZ) + core

    def block_rows(cc, zz):
        return pl.ds(pl.multiple_of((cc * NZ + zz) * tok, tok), tok)

    def slice_y(yy):
        return pl.ds(pl.multiple_of(yy * q, q), q)

    def half_rows(cc):
        return pl.ds(pl.multiple_of(cc * half, half), half)

    barrier = pltpu.get_barrier_semaphore()
    peers = [dict(section=sibling)]
    peers += [dict(tensor=wrap(y + d, NY)) for d in range(1, NY)]
    peers += [dict(section=sibling, tensor=wrap(y + d, NY)) for d in range(1, NY)]
    peers += [dict(section=at_z(z + d)) for d in range(1, NZ)]
    peers += [dict(dp=wrap(x + d, NX)) for d in range(1, NX)]
    for peer in peers:
        pl.semaphore_signal(barrier, inc=1, device_id=peer, device_id_type=pl.DeviceIdType.MESH)
    load_head = pltpu.make_async_copy(head, HEAD, local_sem.at[1])
    load_head.start()
    pl.semaphore_wait(barrier, len(peers))

    own = upd.at[0]

    def ublk(cc, zz, yy):
        return U.at[block_rows(cc, zz), slice_y(yy)]

    keep_own = pltpu.make_async_copy(own, ublk(core, z, y), local_sem.at[2])
    keep_own.start()

    whole = vdev // 16 * 16

    def pad_head(n):
        cols = slice(n * (width // 8), (n + 1) * (width // 8))
        block = HEAD[0:whole, cols]
        H[0:whole, cols] = block
        H[whole:vpad, cols] = jnp.zeros((vpad - whole, width // 8), BF16)
        tail = HEAD[whole:vdev, cols]
        H[whole:vdev, cols] = tail
        HM[n:n + 1, :] = jnp.maximum(
            jnp.max(jnp.abs(block).astype(F32), axis=0, keepdims=True),
            jnp.max(jnp.abs(tail).astype(F32), axis=0, keepdims=True),
        )

    @pl.when(core == 0)
    def _():
        copies = []

        def send(src, dst, ssem, rsem, **device):
            copies.append(copy_to(src, dst, ssem, rsem, **device))
            copies[-1].start()

        def to_sibling(src, zz, yy):
            send(src, ublk(0, zz, yy), s_sib.at[zz, yy], r_sib.at[zz, yy], section=sibling)

        def pass_on(src, zz, yy, k, j, side):
            dst, rsem = ublk(0, zz, yy), r_own.at[zz, yy]
            near = k + 1 < NZ // 2
            last = k + 1 == NZ // 2
            if side != "right" and (near or (last and j < NY // 2)):
                send(src, dst, s_p.at[k, j], rsem, section=at_z(z + 1))
            if side != "left" and (near or (last and j >= NY // 2)):
                send(src, dst, s_m.at[k, j], rsem, section=at_z(z - 1))
            to_sibling(src, zz, yy)

        for n, d in enumerate((2, 1, -1)):
            send(own, ublk(0, z, y), s_y.at[n, 0], r_own.at[z, y], tensor=wrap(y + d, NY))
        pass_on(own, z, y, 0, 0, "here")
        for j in range(1, NY):
            yy = wrap(y + GATHER_Y[j], NY)
            arrived(ublk(0, z, yy), r_own.at[z, yy])
            pass_on(ublk(0, z, yy), z, yy, 0, j, "here")
        load_head.wait()
        for k in range(1, NZ // 2 + 1):
            for j in range(NY):
                yy = wrap(y + GATHER_Y[j], NY)
                for side, d in (("left", -k), ("right", k)):
                    if k == NZ // 2 and (j < NY // 2) != (side == "left"):
                        continue
                    zz = wrap(z + d, NZ)
                    arrived(ublk(0, zz, yy), r_own.at[zz, yy])
                    pass_on(ublk(0, zz, yy), zz, yy, k, j, side)
                if k < 3:
                    pad_head((k - 1) * NY + j)
        for copy in copies:
            copy.wait_send()

    @pl.when(core == 1)
    def _():
        copies = []
        order = (0, -1, 1, -2, 2, -3, 3, -4)

        def send(src, dst, ssem, rsem, **device):
            copies.append(copy_to(src, dst, ssem, rsem, **device))
            copies[-1].start()

        for n, d in enumerate(order):
            zz = wrap(z + d, NZ)
            dst = ublk(1, zz, y)
            src = own if n == 0 else dst
            if n > 0:
                arrived(dst, r_own.at[zz, y])
            if d in (0, -2):
                send(src, dst, s_p.at[-d, 0], r_own.at[zz, y], section=at_z(z + 1))
                send(src, dst, s_p.at[-d, 1], r_own.at[zz, y], section=at_z(z + 2))
            if d in (0, 2):
                send(src, dst, s_m.at[d, 0], r_own.at[zz, y], section=at_z(z - 1))
            if d == 0:
                send(src, dst, s_m.at[d, 1], r_own.at[zz, y], section=at_z(z - 2))
            for m, step in enumerate((1, -1, 2)):
                send(src, dst, s_y.at[m, n], r_own.at[zz, y], tensor=wrap(y + step, NY))
            send(src, dst, s_sib.at[zz, y], r_sib.at[zz, y], section=sibling)
        load_head.wait()
        for n, d in enumerate(order):
            zz = wrap(z + d, NZ)
            for step in (-1, 1, 2):
                yy = wrap(y + step, NY)
                dst = ublk(1, zz, yy)
                arrived(dst, r_own.at[zz, yy])
                send(dst, dst, s_sib.at[zz, yy], r_sib.at[zz, yy], section=sibling)
            pad_head(n)
        for copy in copies:
            copy.wait_send()

    head_top = jnp.max(jnp.max(HM[...], axis=0, keepdims=True), axis=1, keepdims=True)

    def wait_sibling(n, carry):
        zz, yy = lax.div(n, NY), lax.rem(n, NY)
        arrived(ublk(1 - core, zz, yy), r_sib.at[zz, yy])
        return carry

    lax.fori_loop(0, NZ * NY, wait_sibling, 0)
    keep_own.wait()

    chunk = 512
    groups = chunk // 128

    def section_rows(k):
        return pl.ds(((k % 2) * NZ + k // 2) * tok, tok)

    SQ[...] = jnp.zeros_like(SQ)

    def squares(f, carry):
        cols = pl.ds(pl.multiple_of(f * chunk, chunk), chunk)
        hidden = jnp.zeros((tok, chunk), F32)
        for k in range(2 * NZ):
            hidden = hidden + U[section_rows(k), cols].astype(F32)
            square = hidden * hidden
            part = square[:, :128]
            for g in range(1, groups):
                part = part + square[:, g * 128:(g + 1) * 128]
            SQ[section_rows(k), :] += part
        return carry

    def gain_row(f, count):
        return jnp.concatenate([GAIN[pl.ds(f * count + g, 1), :] for g in range(count)], axis=1)

    GAIN[...] = gain[...].astype(F32)
    lax.fori_loop(0, width // chunk, squares, 0)
    mean = jnp.sum(SQ[...], axis=1, keepdims=True) / width
    INV[...] = jnp.broadcast_to(lax.rsqrt(mean + epsilon), (rows, 128))

    def normalize(f, carry):
        cols = pl.ds(pl.multiple_of(f * chunk, chunk), chunk)
        scale = gain_row(f, groups)
        hidden = jnp.zeros((tok, chunk), F32)
        for k in range(2 * NZ):
            hidden = hidden + U[section_rows(k), cols].astype(F32)
            inverse = INV[section_rows(k), :]
            R[section_rows(k), cols] = (
                scale * hidden * jnp.concatenate([inverse] * groups, axis=1)
            ).astype(BF16)
        return carry

    lax.fori_loop(0, width // chunk, normalize, 0)

    part = width // NX

    def slice_x(xx):
        return pl.ds(pl.multiple_of(xx * part, part), part)

    def rx_rows(xx, cc):
        return pl.ds(pl.multiple_of(xx * rows + cc * half, half), half)

    def x_rows(xx):
        return pl.ds(pl.multiple_of(xx * rows, rows), rows)

    row_copies = []
    for n, d in enumerate((1, -1, 2)):
        xx = wrap(x + d, NX)
        row_copies.append(copy_to(
            R.at[half_rows(core), slice_x(xx)], RX.at[rx_rows(x, core), :],
            s_rx.at[n], r_rx.at[x], dp=xx,
        ))
        row_copies[-1].start()
    keep_rows = pltpu.make_async_copy(R.at[:, slice_x(x)], RX.at[x_rows(x), :], local_sem.at[3])
    keep_rows.start()

    depth = 4096
    pad = lax.broadcasted_iota(jnp.int32, (vpad, rows), 0) >= vdev
    L[...] = jnp.where(pad, -1e30, 0.0)

    def logits_step(f, carry):
        cols = pl.ds(pl.multiple_of(f * depth, depth), depth)
        L[...] += lax.dot_general(
            H[:, cols], R[:, cols], (((1,), (1,)), ((), ())), preferred_element_type=F32
        )
        return carry

    lax.fori_loop(0, width // depth, logits_step, 0)

    first = (s * NY + y) * vdev
    column = lax.broadcasted_iota(jnp.int32, (1, rows), 1)
    token = lax.rem(column, tok)
    block = lax.div(column, tok)
    wanted = jnp.zeros((1, rows), jnp.int32)
    for i in range(tok):
        wanted = jnp.where(token == i, targets[i], wanted)
    numerator = jnp.zeros((1, rows), jnp.int32)
    for b in range(2 * NZ):
        numerator = jnp.where(block == b, curriculum[(b % NZ) * 2 + b // NZ], numerator)
    weight = numerator.astype(F32) / scale_denominator
    hit = lax.broadcasted_iota(jnp.int32, (vpad, rows), 0) + first == wanted
    hit = jnp.logical_and(hit, jnp.logical_not(pad))
    logits = L[...]
    top = jnp.max(logits, axis=0, keepdims=True)
    total = jnp.sum(jnp.exp(logits - top), axis=0, keepdims=True)
    target = jnp.sum(jnp.where(hit, logits, 0.0), axis=0, keepdims=True)
    here = core * NY + y
    ST1[here] = jnp.concatenate(
        [top, total, target, jnp.broadcast_to(head_top, (1, rows)), jnp.zeros((4, rows), F32)], axis=0
    )

    def combine(parts):
        top = parts[0][0:1]
        for p in parts[1:]:
            top = jnp.maximum(top, p[0:1])
        total = parts[0][1:2] * jnp.exp(parts[0][0:1] - top)
        target = parts[0][2:3]
        largest = parts[0][3:4]
        for p in parts[1:]:
            largest = jnp.maximum(largest, p[3:4])
            total = total + p[1:2] * jnp.exp(p[0:1] - top)
            target = target + p[2:3]
        return jnp.concatenate([top, total, target, largest, jnp.zeros((4, rows), F32)], axis=0)

    def add_up(parts):
        total = parts[0]
        for p in parts[1:]:
            total = total + p
        return total

    def exchange(level, B1, B2, ssem, r1, r2):
        if level == 1:
            out = [copy_to(B1.at[here], B1.at[here], ssem.at[0], r1.at[here], section=sibling)]
            for n, d in enumerate((1, 3, 2)):
                yy = wrap(y + d, NY)
                out.append(copy_to(B1.at[here], B1.at[here], ssem.at[n + 1], r1.at[here], tensor=yy))
                out.append(copy_to(
                    B1.at[here], B1.at[here], ssem.at[n + NY], r1.at[here], section=sibling, tensor=yy
                ))
        else:
            out = [
                copy_to(B2.at[z], B2.at[z], ssem.at[n + 2 * NY], r2.at[z], section=at_z(z + d))
                for n, d in enumerate((4, 3, 5, 2, 6, 1, 7))
            ]
        for copy in out:
            copy.start()
        return out

    def collect(level, B1, B2, r1, r2):
        if level == 1:
            for cc, d in ((1, 0), (0, 1), (0, 3), (1, 1), (1, 3), (0, 2), (1, 2)):
                slot = lax.rem(core + cc, 2) * NY + wrap(y + d, NY)
                arrived(B1.at[slot], r1.at[slot])
            return [B1[k] for k in range(2 * NY)]
        for d in (1, 7, 2, 6, 3, 5, 4):
            arrived(B2.at[wrap(z + d, NZ)], r2.at[wrap(z + d, NZ)])
        return [B2[k] for k in range(NZ)]

    small = []
    stat_bufs, stat_sems = (ST1, ST2), (r_st1, r_st2)
    small += exchange(1, *stat_bufs, s_st, *stat_sems)
    ST2[z] = combine(collect(1, *stat_bufs, *stat_sems))
    small += exchange(2, *stat_bufs, s_st, *stat_sems)
    final = combine(collect(2, *stat_bufs, *stat_sems))
    lse_row = final[0:1] + jnp.log(final[1:2])
    NL[x] = jnp.broadcast_to(lse_row - final[2:3], (8, rows))
    for n, d in enumerate((1, 2, 3)):
        small.append(copy_to(NL.at[x], NL.at[x], s_nl.at[n], r_nl.at[x], dp=wrap(x + d, NX)))
        small[-1].start()

    logits = L[...]
    probs = jnp.exp(logits - lse_row)
    grad = weight * (probs - jnp.where(hit, 1.0, 0.0))
    rounded = grad.astype(BF16)
    GX[x] = rounded
    GN[...] = jnp.transpose(rounded)
    product = jnp.sum(rounded.astype(F32) * logits, axis=0, keepdims=True)
    CT1[here] = jnp.broadcast_to(product, (8, rows))
    inner_bufs, inner_sems = (CT1, CT2), (r_ct1, r_ct2)
    small += exchange(1, *inner_bufs, s_ct, *inner_sems)
    for n, d in enumerate((1, -1, 2)):
        row_copies.append(copy_to(
            GX.at[x], GX.at[x], s_g.at[n], r_g.at[x], dp=wrap(x + d, NX)
        ))
        row_copies[-1].start()

    later = jnp.zeros((tok, 128), F32)
    for k in reversed(range(2 * NZ)):
        later = later + INV[section_rows(k), :] * (curriculum[k].astype(F32) / scale_denominator)
        bound = jnp.maximum(later * (final[3:4, 0:128] * 2.03), 1e-20)
        BND[section_rows(k), :] = bound
        SC[section_rows(k), :] = (CODE_TOP * CODE_TOP) / bound

    def pair_sum(cc, zz, yy):
        return PB[block_rows(cc, zz), slice_y(yy)] + decode(
            SB[pl.ds(pl.multiple_of(zz * tok, tok), tok), slice_y(yy)]
        )

    def start_coded(value, slot, **device):
        QR[slot] = encode(value)
        copy = copy_to(QR.at[slot], RB.at[slot], s_rs.at[slot], r_rs.at[slot], **device)
        copy.start()
        return copy

    def received(slot):
        arrived(RB.at[slot], r_rs.at[slot])
        return decode(RB[slot])

    def slice_of(j):
        return wrap(y + SCATTER_Y[j], NY)

    up3, down3, far4, up1, down1, up2, down2, over_y = range(0, 8 * NY, NY)
    count = len(SCATTER_Z)
    fourth, third, second, next_up, third_down, second_down, next_down = range(3 * count, 3 * count + 7)

    def first_even(j):
        yy = slice_of(j)
        arrived(SB.at[:, slice_y(yy)], r_sb.at[j])
        way = 2 if j < NY // 2 else -2
        start_coded(pair_sum(0, wrap(z + 4, NZ), yy), far4 + j, section=at_z(z + way))
        start_coded(pair_sum(0, wrap(z + 3, NZ), yy), up3 + j, section=at_z(z + 1))
        start_coded(pair_sum(0, wrap(z - 3, NZ), yy), down3 + j, section=at_z(z - 1))
        start_coded(pair_sum(0, wrap(z + 1, NZ), yy), up1 + j, section=at_z(z + 1))
        start_coded(pair_sum(0, wrap(z - 1, NZ), yy), down1 + j, section=at_z(z - 1))

    def first_odd(j):
        yy = slice_of(j)
        arrived(SB.at[:, slice_y(yy)], r_sb.at[j])
        for n in range(count):
            start_coded(pair_sum(1, wrap(z + SCATTER_Z[n], NZ), yy), j * count + n, tensor=yy)

    def first_step(j):
        pl.when(core == 0)(lambda: first_even(j))
        pl.when(core == 1)(lambda: first_odd(j))

    def sent(slot):
        copy_to(QR.at[slot], RB.at[slot], s_rs.at[slot], r_rs.at[slot], section=sibling).wait_send()

    sib_copies = []
    wide = 1024
    for j in range(NY):
        yy = wrap(y + SCATTER_Y[j], NY)

        def share(f, carry):
            cols = pl.ds(pl.multiple_of(yy * q + f * wide, wide), wide)
            term = jnp.dot(GN[...], H[:, cols], preferred_element_type=F32)
            later = jnp.zeros((tok, wide), F32)
            for k in reversed(range(2 * NZ)):
                at = ((k % 2) * NZ + k // 2) * tok
                inverse = INV[section_rows(k), :]
                later = later + term[at:at + tok] * jnp.concatenate([inverse] * (wide // 128), axis=1)
                PB[section_rows(k), cols] = later * jnp.concatenate([SC[section_rows(k), :]] * (wide // 128), axis=1)
            QS[:, cols] = encode(PB[half_rows(1 - core), cols])
            return carry

        lax.fori_loop(0, q // wide, share, 0)
        sib_copies.append(copy_to(
            QS.at[:, slice_y(yy)], SB.at[:, slice_y(yy)],
            s_sb.at[j], r_sb.at[j], section=sibling,
        ))
        sib_copies[-1].start()
        if j > 0:
            first_step(j - 1)
        if j == 1:
            CT2[z] = add_up(collect(1, *inner_bufs, *inner_sems))
            small += exchange(2, *inner_bufs, s_ct, *inner_sems)

    projected = add_up(collect(2, *inner_bufs, *inner_sems))[0:1]
    projected = jnp.transpose(jnp.broadcast_to(projected, (128, rows)))
    COEF[...] = INV[...] * INV[...] * projected / width

    def second_term(f, carry):
        cols = pl.ds(pl.multiple_of(y * q + f * chunk, chunk), chunk)
        hidden = jnp.zeros((tok, chunk), F32)
        later = jnp.zeros((tok, chunk), F32)
        for k in range(2 * NZ):
            hidden = hidden + U[section_rows(k), cols].astype(F32)
            factor = jnp.where(k >= s, COEF[section_rows(k), :], 0.0)
            later = later + hidden * jnp.concatenate([factor] * groups, axis=1)
        upd_grad[0, :, pl.ds(pl.multiple_of(f * chunk, chunk), chunk)] = later
        return carry

    lax.fori_loop(0, q // chunk, second_term, 0)
    own_gain = gain_row(y, q // 128)

    def pass_rows(copies, d):
        xx = wrap(x + d, NX)
        dst = RX.at[rx_rows(xx, core), :]
        arrived(dst, r_rx.at[xx])
        copies.append(copy_to(dst, dst, s_rxs.at[xx], r_rxs.at[xx], section=sibling))
        copies[-1].start()

    def rows_here():
        for d in (1, -1, 2):
            xx = wrap(x + d, NX)
            arrived(GX.at[xx], r_g.at[xx])
            arrived(RX.at[rx_rows(xx, 1 - core), :], r_rxs.at[xx])

    piece = part // (2 * NX)

    def head_part(f):
        cols = slice(f * piece, (f + 1) * piece)
        total = jnp.zeros((vpad, piece), F32)
        for k in range(NX):
            total = total + jnp.dot(GX[k], RX[k * rows:(k + 1) * rows, cols], preferred_element_type=F32)
        HG[:, cols] = total[0:vdev].astype(BF16)
        out = pltpu.make_async_copy(HG.at[:, cols], head_grad.at[:, cols], s_hg.at[f])
        out.start()
        return out

    keep_rows.wait()

    def write_update(total):
        back = BND[block_rows(core, z), :] / (CODE_TOP * CODE_TOP)
        total = total * jnp.concatenate([back] * (q // 128), axis=1)
        upd_grad[0] = own_gain * total - upd_grad[0]

    @pl.when(core == 0)
    def _():
        copies, outs = [], []

        def second_even(j):
            yy = slice_of(j)
            total = pair_sum(0, wrap(z + 2, NZ), yy) + received(up3 + j)
            if j < NY // 2:
                total = total + received(far4 + j)
            start_coded(total, up2 + j, section=at_z(z + 2))
            total = pair_sum(0, wrap(z - 2, NZ), yy) + received(down3 + j)
            if j >= NY // 2:
                total = total + received(far4 + j)
            start_coded(total, down2 + j, section=at_z(z - 2))

        second_even(0)
        first_even(NY - 1)
        pass_rows(copies, 1)
        pass_rows(copies, -1)
        for j in range(1, NY):
            second_even(j)
        pass_rows(copies, 2)
        for j in range(NY):
            total = pair_sum(0, z, slice_of(j))
            for slot in (up1, down1, up2, down2):
                total = total + received(slot + j)
            if j < NY - 1:
                start_coded(total, over_y + j, tensor=slice_of(j))
        rows_here()
        for n in range(2 * NX):
            outs.append(head_part(n))
        for j in (1, 2, 0):
            total = total + received(over_y + j)
        write_update(total)
        for slot in range(over_y + NY - 1):
            sent(slot)
        for copy in copies:
            copy.wait_send()
        for copy in outs:
            copy.wait()

    @pl.when(core == 1)
    def _():
        copies, outs = [], []
        pass_rows(copies, 1)
        pass_rows(copies, -1)
        arrived(SB.at[:, slice_y(y)], r_sb.at[NY - 1])
        for n, o in enumerate(SCATTER_Z):
            total = pair_sum(1, wrap(z + o, NZ), y)
            for j in range(NY - 1):
                total = total + received(j * count + n)
            if o == 4:
                start_coded(total, fourth, section=at_z(z + 2))
            elif o == 3:
                start_coded(total, third, section=at_z(z + 1))
            elif o == -3:
                start_coded(total, third_down, section=at_z(z - 1))
            elif o == 2:
                start_coded(total + received(fourth) + received(third), second, section=at_z(z + 2))
            elif o == -2:
                start_coded(total + received(third_down), second_down, section=at_z(z - 2))
            elif o == 1:
                start_coded(total, next_up, section=at_z(z + 1))
            elif o == -1:
                start_coded(total, next_down, section=at_z(z - 1))
            if o == -2:
                pass_rows(copies, 2)
        rows_here()
        for n in range(2 * NX):
            outs.append(head_part(n))
        for slot in (next_up, next_down, second, second_down):
            total = total + received(slot)
        write_update(total)
        for slot in range(next_down + 1):
            sent(slot)
        for copy in copies:
            copy.wait_send()
        for copy in outs:
            copy.wait()

    for d in (1, -1, 2):
        xx = wrap(x + d, NX)
        arrived(NL.at[xx], r_nl.at[xx])
    nll = add_up([NL[k] for k in range(NX)])
    nll = jnp.transpose(jnp.broadcast_to(nll[0:1], (128, rows)))
    means = [None] * (2 * NZ)
    for b in range(2 * NZ):
        means[(b % NZ) * 2 + b // NZ] = jnp.sum(
            nll[b * tok:(b + 1) * tok], axis=0, keepdims=True
        ) / (tok * NX)
    means.append(jnp.zeros((128 - 2 * NZ, 128), F32))
    losses[...] = jnp.transpose(jnp.concatenate(means, axis=0))[0:8]

    for copy in row_copies + sib_copies + small:
        copy.wait_send()


def hand_over(upd_in, head_in, losses_in, upd_out, head_out, losses_out, upd_held, head_held, sem):
    count = 4
    step = head_in.shape[1] // count
    pairs = [(upd_in, upd_held, upd_out)]
    for n in range(count):
        cols = pl.ds(n * step, step)
        pairs.append((head_in.at[:, cols], head_held.at[:, cols], head_out.at[:, cols]))
    reads = [pltpu.make_async_copy(a, b, sem.at[0, n]) for n, (a, b, _) in enumerate(pairs)]
    writes = [pltpu.make_async_copy(b, c, sem.at[1, n]) for n, (_, b, c) in enumerate(pairs)]
    for copy in reads:
        copy.start()
    losses_out[...] = losses_in[0:1, 0:2 * NZ]
    for read, write in zip(reads, writes):
        read.wait()
        write.start()
    for copy in writes:
        copy.wait()


def body(updates, norm_gain, head, targets, curriculum):
    _, tok, q = updates.shape
    width, vdev = head.shape
    vpad = (vdev + 15) // 16 * 16
    rows = 2 * NZ * tok
    vmem = pl.BlockSpec(memory_space=pltpu.VMEM)
    smem = pl.BlockSpec(memory_space=pltpu.SMEM)
    hbm = pl.BlockSpec(memory_space=pl.ANY)
    dma = lambda *shape: pltpu.SemaphoreType.DMA(shape)
    slots = NZ * NY + NY
    upd_grad, head_grad, losses = pl.pallas_call(
        kernel,
        out_shape=(
            jax.ShapeDtypeStruct((1, tok, q), F32),
            jax.ShapeDtypeStruct((vdev, width // NX), BF16),
            jax.ShapeDtypeStruct((8, 128), F32),
        ),
        in_specs=[vmem, vmem, hbm, smem, smem],
        out_specs=(vmem, hbm, vmem),
        scratch_shapes=[
            pltpu.VMEM((rows, width), BF16),
            pltpu.VMEM((vdev, width), BF16),
            pltpu.VMEM((vpad, width), BF16),
            pltpu.VMEM((8, width // 8), F32),
            pltpu.VMEM((rows, width), BF16),
            pltpu.VMEM((rows, width), F32),
            pltpu.VMEM((rows // 2, width), jnp.int16),
            pltpu.VMEM((rows // 2, width), jnp.int16),
            pltpu.VMEM((slots, tok, q), jnp.int16),
            pltpu.VMEM((slots, tok, q), jnp.int16),
            pltpu.VMEM((NX * rows, width // NX), BF16),
            pltpu.VMEM((NX, vpad, rows), BF16),
            pltpu.VMEM((rows, vpad), BF16),
            pltpu.VMEM((vpad, rows), F32),
            pltpu.VMEM((width // 128, 128), F32),
            pltpu.VMEM((rows, 128), F32),
            pltpu.VMEM((rows, 128), F32),
            pltpu.VMEM((rows, 128), F32),
            pltpu.VMEM((rows, 128), F32),
            pltpu.VMEM((rows, 128), F32),
            pltpu.VMEM((vdev, width // NX), BF16),
            pltpu.VMEM((2 * NY, 8, rows), F32),
            pltpu.VMEM((NZ, 8, rows), F32),
            pltpu.VMEM((2 * NY, 8, rows), F32),
            pltpu.VMEM((NZ, 8, rows), F32),
            pltpu.VMEM((NX, 8, rows), F32),
            dma(4), dma(NZ, NY), dma(NZ, NY), dma(NZ, NY), dma(NZ, NY), dma(NZ, NY), dma(3, NZ),
            dma(2 * NY + NZ), dma(2 * NY), dma(NZ), dma(2 * NY + NZ), dma(2 * NY), dma(NZ), dma(NX), dma(NX), dma(NX * 2),
            dma(NX), dma(NX), dma(NX), dma(NX), dma(NX), dma(NX), dma(NY), dma(NY), dma(slots), dma(slots),
        ],
        compiler_params=pltpu.CompilerParams(
            collective_id=0, has_side_effects=True, vmem_limit_bytes=60 * 1024 * 1024
        ),
    )(updates, norm_gain.reshape(width // 128, 128), head.T, targets, curriculum)
    upd_grad, head_grad, losses = pl.pallas_call(
        hand_over,
        out_shape=(
            jax.ShapeDtypeStruct(upd_grad.shape, F32),
            jax.ShapeDtypeStruct(head_grad.shape, BF16),
            jax.ShapeDtypeStruct((1, 2 * NZ), F32),
        ),
        in_specs=[hbm, hbm, vmem],
        out_specs=(hbm, hbm, vmem),
        scratch_shapes=[pltpu.VMEM(upd_grad.shape, F32), pltpu.VMEM(head_grad.shape, BF16), dma(2, 5)],
        compiler_params=pltpu.CompilerParams(vmem_limit_bytes=60 * 1024 * 1024),
    )(upd_grad, head_grad, losses)
    return upd_grad, head_grad.T, losses.reshape(2 * NZ)


def solution(mesh):
    return jax.shard_map(
        body,
        mesh=mesh,
        in_specs=(P("section", "dp", "tensor"), P(), P(None, ("section", "tensor")), P("dp"), P()),
        out_specs=(P("section", "dp", "tensor"), P("dp", ("section", "tensor")), P()),
        check_vma=False,
    )
```

```python
import jax
import jax.numpy as jnp
from jax import lax
from jax.experimental import pallas as pl
from jax.experimental.pallas import tpu as pltpu
from jax.sharding import PartitionSpec as P

F32 = jnp.float32
BF16 = jnp.bfloat16
epsilon = 1e-05
scale_denominator = 4.0

NY = 4
NX = 4
NZ = 8

GATHER_Y = (0, -1, 1, 2)
SCATTER_Y = (2, 1, -1, 0)
SCATTER_Z = (4, 3, -3, 2, -2, 1, -1, 0)


def wrap(value, count):
    return lax.rem(value + 2 * count, count)


CODE_TOP = 32766.0


def encode(value):
    root = value * lax.rsqrt(jnp.maximum(jnp.abs(value), 1e-12))
    return jnp.round(root).astype(jnp.int32).astype(jnp.int16)


def decode(code):
    root = code.astype(jnp.int32).astype(F32)
    return root * jnp.abs(root)


def kernel(
    upd, gain, head, targets, curriculum,
    upd_grad, head_grad, losses,
    U, HEAD, H, HM, R, PB, QS, SB, QR, RB, RX, GX, GN, L, GAIN16, GAIN, SQ, INV, COEF, BND, SC, HG, ST1, ST2, CT1, CT2, NL,
    local_sem, r_own, r_sib, s_sib, s_p, s_m, s_y,
    s_st, r_st1, r_st2, s_ct, r_ct1, r_ct2, s_nl, r_nl, s_hg,
    s_rx, r_rx, s_rxs, r_rxs, s_g, r_g, s_sb, r_sb, s_rs, r_rs,
):
    tok, q = upd.shape[1], upd.shape[2]
    width = q * NY
    vdev = head.shape[0]
    vpad = L.shape[0]
    half = NZ * tok
    rows = 2 * half
    s = lax.axis_index("section")
    y = lax.axis_index("tensor")
    x = lax.axis_index("dp")
    core = lax.rem(s, 2)
    z = lax.div(s, 2)
    sibling = s + 1 - 2 * core

    def copy_to(src, dst, ssem, rsem, **device):
        return pltpu.make_async_remote_copy(
            src_ref=src, dst_ref=dst, send_sem=ssem, recv_sem=rsem,
            device_id=device, device_id_type=pl.DeviceIdType.MESH,
        )

    def arrived(dst, rsem):
        copy_to(dst, dst, local_sem.at[0], rsem, section=sibling).wait_recv()

    def at_z(zz):
        return 2 * wrap(zz, NZ) + core

    def block_rows(cc, zz):
        return pl.ds(pl.multiple_of((cc * NZ + zz) * tok, tok), tok)

    def slice_y(yy):
        return pl.ds(pl.multiple_of(yy * q, q), q)

    def half_rows(cc):
        return pl.ds(pl.multiple_of(cc * half, half), half)

    barrier = pltpu.get_barrier_semaphore()
    peers = [dict(section=sibling)]
    peers += [dict(tensor=wrap(y + d, NY)) for d in range(1, NY)]
    peers += [dict(section=sibling, tensor=wrap(y + d, NY)) for d in range(1, NY)]
    peers += [dict(section=at_z(z + d)) for d in range(1, NZ)]
    peers += [dict(dp=wrap(x + d, NX)) for d in range(1, NX)]
    for peer in peers:
        pl.semaphore_signal(barrier, inc=1, device_id=peer, device_id_type=pl.DeviceIdType.MESH)
    load_head = pltpu.make_async_copy(head, HEAD, local_sem.at[1])
    keep_own = pltpu.make_async_copy(upd.at[0], U.at[block_rows(core, z), slice_y(y)], local_sem.at[2])
    keep_own.start()
    load_gain = pltpu.make_async_copy(gain, GAIN16, local_sem.at[4])
    load_gain.start()
    load_head.start()
    pl.semaphore_wait(barrier, len(peers))
    keep_own.wait()

    own = U.at[block_rows(core, z), slice_y(y)]

    def ublk(cc, zz, yy):
        return U.at[block_rows(cc, zz), slice_y(yy)]

    whole = vdev // 16 * 16

    def pad_head(n):
        cols = slice(n * (width // 8), (n + 1) * (width // 8))
        block = HEAD[0:whole, cols]
        H[0:whole, cols] = block
        H[whole:vpad, cols] = jnp.zeros((vpad - whole, width // 8), BF16)
        tail = HEAD[whole:vdev, cols]
        H[whole:vdev, cols] = tail
        HM[n:n + 1, :] = jnp.maximum(
            jnp.max(jnp.abs(block).astype(F32), axis=0, keepdims=True),
            jnp.max(jnp.abs(tail).astype(F32), axis=0, keepdims=True),
        )

    @pl.when(core == 0)
    def _():
        copies = []

        def send(src, dst, ssem, rsem, **device):
            copies.append(copy_to(src, dst, ssem, rsem, **device))
            copies[-1].start()

        def to_sibling(src, zz, yy):
            send(src, ublk(0, zz, yy), s_sib.at[zz, yy], r_sib.at[zz, yy], section=sibling)

        def pass_on(src, zz, yy, k, j, side):
            dst, rsem = ublk(0, zz, yy), r_own.at[zz, yy]
            near = k + 1 < NZ // 2
            last = k + 1 == NZ // 2
            if side != "right" and (near or (last and j < NY // 2)):
                send(src, dst, s_p.at[k, j], rsem, section=at_z(z + 1))
            if side != "left" and (near or (last and j >= NY // 2)):
                send(src, dst, s_m.at[k, j], rsem, section=at_z(z - 1))
            to_sibling(src, zz, yy)

        for n, d in enumerate((2, 1, -1)):
            send(own, ublk(0, z, y), s_y.at[n, 0], r_own.at[z, y], tensor=wrap(y + d, NY))
        pass_on(own, z, y, 0, 0, "here")
        for j in range(1, NY):
            yy = wrap(y + GATHER_Y[j], NY)
            arrived(ublk(0, z, yy), r_own.at[z, yy])
            pass_on(ublk(0, z, yy), z, yy, 0, j, "here")
        load_head.wait()
        for k in range(1, NZ // 2 + 1):
            for j in range(NY):
                yy = wrap(y + GATHER_Y[j], NY)
                for side, d in (("left", -k), ("right", k)):
                    if k == NZ // 2 and (j < NY // 2) != (side == "left"):
                        continue
                    zz = wrap(z + d, NZ)
                    arrived(ublk(0, zz, yy), r_own.at[zz, yy])
                    pass_on(ublk(0, zz, yy), zz, yy, k, j, side)
                if k < 3:
                    pad_head((k - 1) * NY + j)
        for copy in copies:
            copy.wait_send()

    @pl.when(core == 1)
    def _():
        copies = []
        order = (0, -2, 2, -1, 1, -3, 3, -4)

        def send(src, dst, ssem, rsem, **device):
            copies.append(copy_to(src, dst, ssem, rsem, **device))
            copies[-1].start()

        for n, d in enumerate(order):
            zz = wrap(z + d, NZ)
            dst = ublk(1, zz, y)
            src = own if n == 0 else dst
            if n > 0:
                arrived(dst, r_own.at[zz, y])
            if d in (0, -2):
                send(src, dst, s_p.at[-d, 0], r_own.at[zz, y], section=at_z(z + 1))
                send(src, dst, s_p.at[-d, 1], r_own.at[zz, y], section=at_z(z + 2))
            if d in (0, 2):
                send(src, dst, s_m.at[d, 0], r_own.at[zz, y], section=at_z(z - 1))
            if d == 0:
                send(src, dst, s_m.at[d, 1], r_own.at[zz, y], section=at_z(z - 2))
            for m, step in enumerate((1, -1, 2)):
                send(src, dst, s_y.at[m, n], r_own.at[zz, y], tensor=wrap(y + step, NY))
            send(src, dst, s_sib.at[zz, y], r_sib.at[zz, y], section=sibling)
        load_head.wait()
        for n, d in enumerate(order):
            zz = wrap(z + d, NZ)
            for step in (-1, 1, 2):
                yy = wrap(y + step, NY)
                dst = ublk(1, zz, yy)
                arrived(dst, r_own.at[zz, yy])
                send(dst, dst, s_sib.at[zz, yy], r_sib.at[zz, yy], section=sibling)
            pad_head(n)
        for copy in copies:
            copy.wait_send()

    head_top = jnp.max(jnp.max(HM[...], axis=0, keepdims=True), axis=1, keepdims=True)

    def wait_sibling(n, carry):
        zz, yy = lax.div(n, NY), lax.rem(n, NY)
        arrived(ublk(1 - core, zz, yy), r_sib.at[zz, yy])
        return carry

    lax.fori_loop(0, NZ * NY, wait_sibling, 0)

    chunk = 512
    groups = chunk // 128

    def section_rows(k):
        return pl.ds(((k % 2) * NZ + k // 2) * tok, tok)

    SQ[...] = jnp.zeros_like(SQ)

    def squares(f, carry):
        cols = pl.ds(pl.multiple_of(f * chunk, chunk), chunk)
        hidden = jnp.zeros((tok, chunk), F32)
        for k in range(2 * NZ):
            hidden = hidden + U[section_rows(k), cols].astype(F32)
            square = hidden * hidden
            part = square[:, :128]
            for g in range(1, groups):
                part = part + square[:, g * 128:(g + 1) * 128]
            SQ[section_rows(k), :] += part
        return carry

    def gain_row(f, count):
        return jnp.concatenate([GAIN[pl.ds(f * count + g, 1), :] for g in range(count)], axis=1)

    load_gain.wait()
    GAIN[...] = GAIN16[...].astype(F32)
    lax.fori_loop(0, width // chunk, squares, 0)
    mean = jnp.sum(SQ[...], axis=1, keepdims=True) / width
    INV[...] = jnp.broadcast_to(lax.rsqrt(mean + epsilon), (rows, 128))

    def normalize(f, carry):
        cols = pl.ds(pl.multiple_of(f * chunk, chunk), chunk)
        scale = gain_row(f, groups)
        hidden = jnp.zeros((tok, chunk), F32)
        for k in range(2 * NZ):
            hidden = hidden + U[section_rows(k), cols].astype(F32)
            inverse = INV[section_rows(k), :]
            R[section_rows(k), cols] = (
                scale * hidden * jnp.concatenate([inverse] * groups, axis=1)
            ).astype(BF16)
        return carry

    lax.fori_loop(0, width // chunk, normalize, 0)

    part = width // NX

    def slice_x(xx):
        return pl.ds(pl.multiple_of(xx * part, part), part)

    def rx_rows(xx, cc):
        return pl.ds(pl.multiple_of(xx * rows + cc * half, half), half)

    def x_rows(xx):
        return pl.ds(pl.multiple_of(xx * rows, rows), rows)

    row_copies = []
    for n, d in enumerate((1, -1, 2)):
        xx = wrap(x + d, NX)
        row_copies.append(copy_to(
            R.at[half_rows(core), slice_x(xx)], RX.at[rx_rows(x, core), :],
            s_rx.at[n], r_rx.at[x], dp=xx,
        ))
        row_copies[-1].start()
    keep_rows = pltpu.make_async_copy(R.at[:, slice_x(x)], RX.at[x_rows(x), :], local_sem.at[3])
    keep_rows.start()

    depth = 4096
    pad = lax.broadcasted_iota(jnp.int32, (vpad, rows), 0) >= vdev
    L[...] = jnp.where(pad, -1e30, 0.0)

    def logits_step(f, carry):
        cols = pl.ds(pl.multiple_of(f * depth, depth), depth)
        L[...] += lax.dot_general(
            H[:, cols], R[:, cols], (((1,), (1,)), ((), ())), preferred_element_type=F32
        )
        return carry

    lax.fori_loop(0, width // depth, logits_step, 0)

    first = (s * NY + y) * vdev
    column = lax.broadcasted_iota(jnp.int32, (1, rows), 1)
    token = lax.rem(column, tok)
    block = lax.div(column, tok)
    wanted = jnp.zeros((1, rows), jnp.int32)
    for i in range(tok):
        wanted = jnp.where(token == i, targets[i], wanted)
    numerator = jnp.zeros((1, rows), jnp.int32)
    for b in range(2 * NZ):
        numerator = jnp.where(block == b, curriculum[(b % NZ) * 2 + b // NZ], numerator)
    weight = numerator.astype(F32) / scale_denominator
    hit = lax.broadcasted_iota(jnp.int32, (vpad, rows), 0) + first == wanted
    hit = jnp.logical_and(hit, jnp.logical_not(pad))
    logits = L[...]
    top = jnp.max(logits, axis=0, keepdims=True)
    total = jnp.sum(jnp.exp(logits - top), axis=0, keepdims=True)
    target = jnp.sum(jnp.where(hit, logits, 0.0), axis=0, keepdims=True)
    here = core * NY + y
    ST1[here] = jnp.concatenate(
        [top, total, target, jnp.broadcast_to(head_top, (1, rows)), jnp.zeros((4, rows), F32)], axis=0
    )

    def combine(parts):
        top = parts[0][0:1]
        for p in parts[1:]:
            top = jnp.maximum(top, p[0:1])
        total = parts[0][1:2] * jnp.exp(parts[0][0:1] - top)
        target = parts[0][2:3]
        largest = parts[0][3:4]
        for p in parts[1:]:
            largest = jnp.maximum(largest, p[3:4])
            total = total + p[1:2] * jnp.exp(p[0:1] - top)
            target = target + p[2:3]
        return jnp.concatenate([top, total, target, largest, jnp.zeros((4, rows), F32)], axis=0)

    def add_up(parts):
        total = parts[0]
        for p in parts[1:]:
            total = total + p
        return total

    def exchange(level, B1, B2, ssem, r1, r2):
        if level == 1:
            out = [copy_to(B1.at[here], B1.at[here], ssem.at[0], r1.at[here], section=sibling)]
            for n, d in enumerate((1, 3, 2)):
                yy = wrap(y + d, NY)
                out.append(copy_to(B1.at[here], B1.at[here], ssem.at[n + 1], r1.at[here], tensor=yy))
                out.append(copy_to(
                    B1.at[here], B1.at[here], ssem.at[n + NY], r1.at[here], section=sibling, tensor=yy
                ))
        else:
            out = [
                copy_to(B2.at[z], B2.at[z], ssem.at[n + 2 * NY], r2.at[z], section=at_z(z + d))
                for n, d in enumerate((4, 3, 5, 2, 6, 1, 7))
            ]
        for copy in out:
            copy.start()
        return out

    def collect(level, B1, B2, r1, r2):
        if level == 1:
            for cc, d in ((1, 0), (0, 1), (0, 3), (1, 1), (1, 3), (0, 2), (1, 2)):
                slot = lax.rem(core + cc, 2) * NY + wrap(y + d, NY)
                arrived(B1.at[slot], r1.at[slot])
            return [B1[k] for k in range(2 * NY)]
        for d in (1, 7, 2, 6, 3, 5, 4):
            arrived(B2.at[wrap(z + d, NZ)], r2.at[wrap(z + d, NZ)])
        return [B2[k] for k in range(NZ)]

    small = []
    stat_bufs, stat_sems = (ST1, ST2), (r_st1, r_st2)
    small += exchange(1, *stat_bufs, s_st, *stat_sems)
    ST2[z] = combine(collect(1, *stat_bufs, *stat_sems))
    small += exchange(2, *stat_bufs, s_st, *stat_sems)
    final = combine(collect(2, *stat_bufs, *stat_sems))
    lse_row = final[0:1] + jnp.log(final[1:2])
    NL[x] = jnp.broadcast_to(lse_row - final[2:3], (8, rows))
    for n, d in enumerate((1, 2, 3)):
        small.append(copy_to(NL.at[x], NL.at[x], s_nl.at[n], r_nl.at[x], dp=wrap(x + d, NX)))
        small[-1].start()

    logits = L[...]
    probs = jnp.exp(logits - lse_row)
    grad = weight * (probs - jnp.where(hit, 1.0, 0.0))
    rounded = grad.astype(BF16)
    GX[x] = rounded
    GN[...] = jnp.transpose(rounded)
    product = jnp.sum(rounded.astype(F32) * logits, axis=0, keepdims=True)
    CT1[here] = jnp.broadcast_to(product, (8, rows))
    inner_bufs, inner_sems = (CT1, CT2), (r_ct1, r_ct2)
    small += exchange(1, *inner_bufs, s_ct, *inner_sems)
    for n, d in enumerate((1, -1, 2)):
        row_copies.append(copy_to(
            GX.at[x], GX.at[x], s_g.at[n], r_g.at[x], dp=wrap(x + d, NX)
        ))
        row_copies[-1].start()

    later = jnp.zeros((tok, 128), F32)
    for k in reversed(range(2 * NZ)):
        later = later + INV[section_rows(k), :] * (curriculum[k].astype(F32) / scale_denominator)
        bound = jnp.maximum(later * (final[3:4, 0:128] * 2.03), 1e-20)
        BND[section_rows(k), :] = bound
        SC[section_rows(k), :] = (CODE_TOP * CODE_TOP) / bound

    def pair_sum(cc, zz, yy):
        return PB[block_rows(cc, zz), slice_y(yy)] + decode(
            SB[pl.ds(pl.multiple_of(zz * tok, tok), tok), slice_y(yy)]
        )

    def start_coded(value, slot, **device):
        QR[slot] = encode(value)
        copy = copy_to(QR.at[slot], RB.at[slot], s_rs.at[slot], r_rs.at[slot], **device)
        copy.start()
        return copy

    def received(slot):
        arrived(RB.at[slot], r_rs.at[slot])
        return decode(RB[slot])

    def slice_of(j):
        return wrap(y + SCATTER_Y[j], NY)

    up3, down3, far4, up1, down1, up2, down2, over_y = range(0, 8 * NY, NY)
    count = len(SCATTER_Z)
    fourth, third, second, next_up, third_down, second_down, next_down = range(3 * count, 3 * count + 7)

    def first_even(j):
        yy = slice_of(j)
        arrived(SB.at[:, slice_y(yy)], r_sb.at[j])
        way = 2 if j < NY // 2 else -2
        start_coded(pair_sum(0, wrap(z + 4, NZ), yy), far4 + j, section=at_z(z + way))
        start_coded(pair_sum(0, wrap(z + 3, NZ), yy), up3 + j, section=at_z(z + 1))
        start_coded(pair_sum(0, wrap(z - 3, NZ), yy), down3 + j, section=at_z(z - 1))
        start_coded(pair_sum(0, wrap(z + 1, NZ), yy), up1 + j, section=at_z(z + 1))
        start_coded(pair_sum(0, wrap(z - 1, NZ), yy), down1 + j, section=at_z(z - 1))

    def first_odd(j):
        yy = slice_of(j)
        arrived(SB.at[:, slice_y(yy)], r_sb.at[j])
        for n in range(count):
            start_coded(pair_sum(1, wrap(z + SCATTER_Z[n], NZ), yy), j * count + n, tensor=yy)

    def first_step(j):
        pl.when(core == 0)(lambda: first_even(j))
        pl.when(core == 1)(lambda: first_odd(j))

    def sent(slot):
        copy_to(QR.at[slot], RB.at[slot], s_rs.at[slot], r_rs.at[slot], section=sibling).wait_send()

    sib_copies = []
    wide = 1024
    for j in range(NY):
        yy = wrap(y + SCATTER_Y[j], NY)

        def share(f, carry):
            cols = pl.ds(pl.multiple_of(yy * q + f * wide, wide), wide)
            term = jnp.dot(GN[...], H[:, cols], preferred_element_type=F32)
            later = jnp.zeros((tok, wide), F32)
            for k in reversed(range(2 * NZ)):
                at = ((k % 2) * NZ + k // 2) * tok
                inverse = INV[section_rows(k), :]
                later = later + term[at:at + tok] * jnp.concatenate([inverse] * (wide // 128), axis=1)
                PB[section_rows(k), cols] = later * jnp.concatenate([SC[section_rows(k), :]] * (wide // 128), axis=1)
            QS[:, cols] = encode(PB[half_rows(1 - core), cols])
            return carry

        lax.fori_loop(0, q // wide, share, 0)
        sib_copies.append(copy_to(
            QS.at[:, slice_y(yy)], SB.at[:, slice_y(yy)],
            s_sb.at[j], r_sb.at[j], section=sibling,
        ))
        sib_copies[-1].start()
        if j > 0:
            first_step(j - 1)
        if j == 1:
            CT2[z] = add_up(collect(1, *inner_bufs, *inner_sems))
            small += exchange(2, *inner_bufs, s_ct, *inner_sems)

    projected = add_up(collect(2, *inner_bufs, *inner_sems))[0:1]
    projected = jnp.transpose(jnp.broadcast_to(projected, (128, rows)))
    COEF[...] = INV[...] * INV[...] * projected / width

    def second_term(f, carry):
        cols = pl.ds(pl.multiple_of(y * q + f * chunk, chunk), chunk)
        hidden = jnp.zeros((tok, chunk), F32)
        later = jnp.zeros((tok, chunk), F32)
        for k in range(2 * NZ):
            hidden = hidden + U[section_rows(k), cols].astype(F32)
            factor = jnp.where(k >= s, COEF[section_rows(k), :], 0.0)
            later = later + hidden * jnp.concatenate([factor] * groups, axis=1)
        upd_grad[0, :, pl.ds(pl.multiple_of(f * chunk, chunk), chunk)] = later
        return carry

    lax.fori_loop(0, q // chunk, second_term, 0)
    own_gain = gain_row(y, q // 128)

    def pass_rows(copies, d):
        xx = wrap(x + d, NX)
        dst = RX.at[rx_rows(xx, core), :]
        arrived(dst, r_rx.at[xx])
        copies.append(copy_to(dst, dst, s_rxs.at[xx], r_rxs.at[xx], section=sibling))
        copies[-1].start()

    def rows_here():
        for d in (1, -1, 2):
            xx = wrap(x + d, NX)
            arrived(GX.at[xx], r_g.at[xx])
            arrived(RX.at[rx_rows(xx, 1 - core), :], r_rxs.at[xx])

    piece = part // (2 * NX)

    def head_part(f):
        cols = slice(f * piece, (f + 1) * piece)
        total = jnp.zeros((vpad, piece), F32)
        for k in range(NX):
            total = total + jnp.dot(GX[k], RX[k * rows:(k + 1) * rows, cols], preferred_element_type=F32)
        HG[:, cols] = total[0:vdev].astype(BF16)
        out = pltpu.make_async_copy(HG.at[:, cols], head_grad.at[:, cols], s_hg.at[f])
        out.start()
        return out

    keep_rows.wait()

    def write_update(total):
        back = BND[block_rows(core, z), :] / (CODE_TOP * CODE_TOP)
        total = total * jnp.concatenate([back] * (q // 128), axis=1)
        upd_grad[0] = own_gain * total - upd_grad[0]

    @pl.when(core == 0)
    def _():
        copies, outs = [], []

        def second_even(j):
            yy = slice_of(j)
            total = pair_sum(0, wrap(z + 2, NZ), yy) + received(up3 + j)
            if j < NY // 2:
                total = total + received(far4 + j)
            start_coded(total, up2 + j, section=at_z(z + 2))
            total = pair_sum(0, wrap(z - 2, NZ), yy) + received(down3 + j)
            if j >= NY // 2:
                total = total + received(far4 + j)
            start_coded(total, down2 + j, section=at_z(z - 2))

        second_even(0)
        first_even(NY - 1)
        pass_rows(copies, 1)
        pass_rows(copies, -1)
        for j in range(1, NY):
            second_even(j)
        pass_rows(copies, 2)
        for j in range(NY):
            total = pair_sum(0, z, slice_of(j))
            for slot in (up1, down1, up2, down2):
                total = total + received(slot + j)
            if j < NY - 1:
                start_coded(total, over_y + j, tensor=slice_of(j))
        rows_here()
        for n in range(2 * NX):
            outs.append(head_part(n))
        for j in (1, 2, 0):
            total = total + received(over_y + j)
        write_update(total)
        for slot in range(over_y + NY - 1):
            sent(slot)
        for copy in copies:
            copy.wait_send()
        for copy in outs:
            copy.wait()

    @pl.when(core == 1)
    def _():
        copies, outs = [], []
        pass_rows(copies, 1)
        pass_rows(copies, -1)
        arrived(SB.at[:, slice_y(y)], r_sb.at[NY - 1])
        for n, o in enumerate(SCATTER_Z):
            total = pair_sum(1, wrap(z + o, NZ), y)
            for j in range(NY - 1):
                total = total + received(j * count + n)
            if o == 4:
                start_coded(total, fourth, section=at_z(z + 2))
            elif o == 3:
                start_coded(total, third, section=at_z(z + 1))
            elif o == -3:
                start_coded(total, third_down, section=at_z(z - 1))
            elif o == 2:
                start_coded(total + received(fourth) + received(third), second, section=at_z(z + 2))
            elif o == -2:
                start_coded(total + received(third_down), second_down, section=at_z(z - 2))
            elif o == 1:
                start_coded(total, next_up, section=at_z(z + 1))
            elif o == -1:
                start_coded(total, next_down, section=at_z(z - 1))
            if o == -2:
                pass_rows(copies, 2)
        rows_here()
        for n in range(2 * NX):
            outs.append(head_part(n))
        for slot in (next_up, next_down, second, second_down):
            total = total + received(slot)
        write_update(total)
        for slot in range(next_down + 1):
            sent(slot)
        for copy in copies:
            copy.wait_send()
        for copy in outs:
            copy.wait()

    for d in (1, -1, 2):
        xx = wrap(x + d, NX)
        arrived(NL.at[xx], r_nl.at[xx])
    nll = add_up([NL[k] for k in range(NX)])
    nll = jnp.transpose(jnp.broadcast_to(nll[0:1], (128, rows)))
    means = [None] * (2 * NZ)
    for b in range(2 * NZ):
        means[(b % NZ) * 2 + b // NZ] = jnp.sum(
            nll[b * tok:(b + 1) * tok], axis=0, keepdims=True
        ) / (tok * NX)
    means.append(jnp.zeros((128 - 2 * NZ, 128), F32))
    losses[...] = jnp.transpose(jnp.concatenate(means, axis=0))[0:8]

    for copy in row_copies + sib_copies + small:
        copy.wait_send()


def hand_over(upd_in, head_in, losses_in, upd_out, head_out, losses_out, upd_held, head_held, held, row, sem):
    count = 4
    step = head_in.shape[1] // count
    pairs = [(upd_in, upd_held, upd_out)]
    for n in range(count):
        cols = pl.ds(n * step, step)
        pairs.append((head_in.at[:, cols], head_held.at[:, cols], head_out.at[:, cols]))
    reads = [pltpu.make_async_copy(a, b, sem.at[0, n]) for n, (a, b, _) in enumerate(pairs)]
    writes = [pltpu.make_async_copy(b, c, sem.at[1, n]) for n, (_, b, c) in enumerate(pairs)]
    read_row = pltpu.make_async_copy(losses_in, held, sem.at[0, count + 1])
    write_row = pltpu.make_async_copy(row, losses_out, sem.at[1, count + 1])
    read_row.start()
    for copy in reads:
        copy.start()
    read_row.wait()
    row[...] = held[0:1, 0:2 * NZ]
    write_row.start()
    for read, write in zip(reads, writes):
        read.wait()
        write.start()
    for copy in writes + [write_row]:
        copy.wait()


def body(updates, norm_gain, head, targets, curriculum):
    _, tok, q = updates.shape
    width, vdev = head.shape
    vpad = (vdev + 15) // 16 * 16
    rows = 2 * NZ * tok
    vmem = pl.BlockSpec(memory_space=pltpu.VMEM)
    smem = pl.BlockSpec(memory_space=pltpu.SMEM)
    hbm = pl.BlockSpec(memory_space=pl.ANY)
    dma = lambda *shape: pltpu.SemaphoreType.DMA(shape)
    slots = NZ * NY + NY
    upd_grad, head_grad, losses = pl.pallas_call(
        kernel,
        out_shape=(
            jax.ShapeDtypeStruct((1, tok, q), F32),
            jax.ShapeDtypeStruct((vdev, width // NX), BF16),
            jax.ShapeDtypeStruct((8, 128), F32),
        ),
        in_specs=[hbm, hbm, hbm, smem, smem],
        out_specs=(vmem, hbm, vmem),
        scratch_shapes=[
            pltpu.VMEM((rows, width), BF16),
            pltpu.VMEM((vdev, width), BF16),
            pltpu.VMEM((vpad, width), BF16),
            pltpu.VMEM((8, width // 8), F32),
            pltpu.VMEM((rows, width), BF16),
            pltpu.VMEM((rows, width), F32),
            pltpu.VMEM((rows // 2, width), jnp.int16),
            pltpu.VMEM((rows // 2, width), jnp.int16),
            pltpu.VMEM((slots, tok, q), jnp.int16),
            pltpu.VMEM((slots, tok, q), jnp.int16),
            pltpu.VMEM((NX * rows, width // NX), BF16),
            pltpu.VMEM((NX, vpad, rows), BF16),
            pltpu.VMEM((rows, vpad), BF16),
            pltpu.VMEM((vpad, rows), F32),
            pltpu.VMEM((width // 128, 128), BF16),
            pltpu.VMEM((width // 128, 128), F32),
            pltpu.VMEM((rows, 128), F32),
            pltpu.VMEM((rows, 128), F32),
            pltpu.VMEM((rows, 128), F32),
            pltpu.VMEM((rows, 128), F32),
            pltpu.VMEM((rows, 128), F32),
            pltpu.VMEM((vdev, width // NX), BF16),
            pltpu.VMEM((2 * NY, 8, rows), F32),
            pltpu.VMEM((NZ, 8, rows), F32),
            pltpu.VMEM((2 * NY, 8, rows), F32),
            pltpu.VMEM((NZ, 8, rows), F32),
            pltpu.VMEM((NX, 8, rows), F32),
            dma(5), dma(NZ, NY), dma(NZ, NY), dma(NZ, NY), dma(NZ, NY), dma(NZ, NY), dma(3, NZ),
            dma(2 * NY + NZ), dma(2 * NY), dma(NZ), dma(2 * NY + NZ), dma(2 * NY), dma(NZ), dma(NX), dma(NX), dma(NX * 2),
            dma(NX), dma(NX), dma(NX), dma(NX), dma(NX), dma(NX), dma(NY), dma(NY), dma(slots), dma(slots),
        ],
        compiler_params=pltpu.CompilerParams(
            collective_id=0, has_side_effects=True, vmem_limit_bytes=60 * 1024 * 1024
        ),
    )(updates, norm_gain.reshape(width // 128, 128), head.T, targets, curriculum)
    upd_grad, head_grad, losses = pl.pallas_call(
        hand_over,
        out_shape=(
            jax.ShapeDtypeStruct(upd_grad.shape, F32),
            jax.ShapeDtypeStruct(head_grad.shape, BF16),
            jax.ShapeDtypeStruct((1, 2 * NZ), F32),
        ),
        in_specs=[hbm, hbm, hbm],
        out_specs=(hbm, hbm, hbm),
        scratch_shapes=[
            pltpu.VMEM(upd_grad.shape, F32), pltpu.VMEM(head_grad.shape, BF16),
            pltpu.VMEM((8, 128), F32), pltpu.VMEM((1, 2 * NZ), F32), dma(2, 6),
        ],
        compiler_params=pltpu.CompilerParams(vmem_limit_bytes=60 * 1024 * 1024),
    )(upd_grad, head_grad, losses)
    return upd_grad, head_grad.T, losses.reshape(2 * NZ)


def solution(mesh):
    return jax.shard_map(
        body,
        mesh=mesh,
        in_specs=(P("section", "dp", "tensor"), P(), P(None, ("section", "tensor")), P("dp"), P()),
        out_specs=(P("section", "dp", "tensor"), P("dp", ("section", "tensor")), P()),
        check_vma=False,
    )
```
